256 devices in a mesh: area: 32 (over z, x), row: 8 (over y, core).
Axes of the slice: x: 4, y: 4, z: 8, core: 2. Of those that a mesh axis runs over, the one named last changes fastest.
Arguments:
- conductance_inverse: float32 [256, 1024, 1024], P(('area', 'row')), as said below
- cap_history: float32 [256, 1024, 128], P(('area', 'row')), may hold values from -3 to 3
- cap_conductance: float32 [256, 1024], P(('area', 'row')), may hold values from 0.5 to 0.8
- wave_history: float32 [256, 40, 32, 128], P(('area', 'row')), may hold values from -6 to 6
- line_partner: int32 [256, 32], P(('area', 'row')), may hold values from 0 to 255, as said below
- line_node: int32 [256, 32], P(('area', 'row')), may hold values from 0 to 1023
- line_delay: int32 [256, 32], P(('area', 'row')), may hold values from 20 to 40
- line_admittance: float32 [256, 32], P(('area', 'row')), may hold values from 0.2 to 1
- conv_node: int32 [256, 64], P(('area', 'row')), may hold values from 0 to 1023
- conv_count: int32 [256], P(('area', 'row')), may hold values from 1 to 64, as said below
- conv_state: float32 [256, 2, 64, 128], P(('area', 'row')), may hold values from -3 to 3
- conv_reference: float32 [256, 2, 64, 128], P(('area', 'row')), may hold values from -4 to 4
- conv_rate: float32 [256, 64], P(('area', 'row')), may hold values from 0.03 to 0.6
- conv_limit: float32 [256, 64], P(('area', 'row')), may hold values from 1 to 2.5
- port_node: int32 [256, 8], P(('area', 'row')), may hold values from 0 to 1023
- port_admittance: float32 [256, 8], P(('area', 'row')), may hold values from 0.3 to 1.2
- port_voltage_prev: float32 [2, 256, 8, 128], P(None, ('area', 'row')), may hold values from -5 to 5
- port_bus: int32 [256, 8], P('area'), may hold values from 0 to 20479
- transfer_impedance: float32 [2, 20480, 2048], P(None, 'row', 'area'), may hold values from -0.25 to 0.25
Outputs:
- waves: float32 [256, 20, 32, 128], P(('area', 'row'))
- cap_history_out: float32 [256, 1024, 128], P(('area', 'row'))
- conv_state_out: float32 [256, 2, 64, 128], P(('area', 'row'))
- bus_voltage: float32 [2, 20480, 128], P(None, 'row')
- port_voltage: float32 [2, 256, 8, 128], P(None, ('area', 'row'))
The draws below stay inside these ranges and needn't reach their ends.
Inputs may be any that keep to these rules, and one draw needn't show every extreme that they name: Slot l < 16 of subnetwork s and slot l + 16 of subnetwork (s + k_l) mod 256 are the two ends of one line, with k_l in 1 or 2 the same for every subnetwork and exactly 12 of the k_l equal to 1; so line_partner[s, l] = (s + k_l) mod 256 and line_partner[s, l + 16] = (s - k_l) mod 256. `conv_count`: some subnetwork has all 64 converters in service. `conductance_inverse`: each subnetwork's inverse nodal conductance matrix.
All inputs are finite; a program needn't handle non-finite values.
Results may differ from the reference program's by a relative error of at most 0.0003.
Values sent between devices are 32-bit elements; how exact they have to be, the bound alone decides.
No kernel may reach another device: no remote copies, remote signals or barrier semaphores. Data moves between devices by JAX's collectives and lax.ppermute only.
A program may use at most 64 MiB of HBM per device.

```python
import math
import jax
import jax.numpy as jnp
from jax import lax

NODES = 1024
CASES = 128
STEPS = 20
HIST = 40
LINES = 32
NEAR = 12
CONV = 64
PORTS = 8
NB = 20480
SUBNETS = 256
NPORT = 2048


def draw_conductance_inverse(key, part):
    first, second = jax.random.split(key)
    diagonal = 0.5 + 0.4 * jax.random.uniform(first, (SUBNETS, NODES), dtype=jnp.float32)
    spread = jax.random.normal(second, (SUBNETS, NODES, NODES), dtype=jnp.float32) * (0.2 / NODES ** 0.5)
    return spread + diagonal[:, :, None] * jnp.eye(NODES, dtype=jnp.float32)[None, :, :]


def draw_line_partner(key, part):
    order = jax.random.permutation(jax.random.fold_in(key, 11), LINES // 2)
    reach = jnp.where(order < NEAR, 1, 2).astype(jnp.int32)
    subnet = jnp.arange(SUBNETS, dtype=jnp.int32)[:, None]
    upper = (subnet + reach[None, :]) % SUBNETS
    lower = (subnet - reach[None, :]) % SUBNETS
    return jnp.concatenate([upper, lower], axis=1).astype(jnp.int32)


def draw_conv_count(key, part):
    first, second = jax.random.split(jax.random.fold_in(key, 23))
    counts = jax.random.randint(first, (SUBNETS,), 1, CONV + 1, dtype=jnp.int32)
    where_full = jax.random.randint(second, (), 0, SUBNETS, dtype=jnp.int32)
    return counts.at[where_full].set(CONV).astype(jnp.int32)


def place_ends(result, rng, least, top_value):
    extent = result.shape
    place = [jax.random.randint(jax.random.fold_in(rng, axis), (), 0, extent[axis]) for axis in range(len(extent))]
    result = result.at[tuple(place)].set(least)
    longest = extent.index(max(extent))
    place[longest] = (place[longest] + 1) % extent[longest]
    return result.at[tuple(place)].set(top_value)


def block_levels(key, extent, pieces, low, top_value):
    def one(dim, parts):
        steps = jax.random.uniform(jax.random.fold_in(jax.random.fold_in(key, 6), dim), (parts,), jnp.float32, low / len(pieces), top_value / len(pieces))
        return jnp.repeat(jnp.exp(steps), extent[dim] // parts).reshape((-1,) + (1,) * (len(extent) - dim - 1))

    gain = one(*pieces[0])
    for cut in pieces[1:]:
        gain = gain * one(*cut)
    return gain


def noise(rng, extent, deviation, most, cuts=(), held_as=jnp.bfloat16):
    values = jax.random.normal(rng, extent, jnp.float32) * deviation
    if len(cuts) > 0:
        values = block_levels(rng, extent, cuts, -0.22, 0.18) * values
    return jnp.clip(values, min=-most, max=most).astype(held_as)


def setup_inputs(seed: int = 0) -> dict:
    streams_of = jax.random.split(jax.random.key(seed), 20)
    return {
        "conductance_inverse": draw_conductance_inverse(jax.random.fold_in(streams_of[19], 71), 0),
        "cap_history": noise(streams_of[1], (SUBNETS, NODES, CASES), 0.5, 3.0, ((0, 256),), jnp.float32),
        "cap_conductance": jnp.clip(0.5 + 0.3 * jax.random.uniform(streams_of[2], (SUBNETS, NODES), jnp.float32) ** block_levels(streams_of[2], (SUBNETS, NODES), ((0, 256),), -0.2, 0.2), 0.5, 0.8),
        "wave_history": noise(streams_of[3], (SUBNETS, HIST, LINES, CASES), 1.0, 6.0, ((0, 256),), jnp.float32),
        "line_partner": draw_line_partner(jax.random.fold_in(streams_of[19], 71), 0),
        "line_node": place_ends(jax.random.randint(streams_of[5], (SUBNETS, LINES), 0, NODES), jax.random.fold_in(streams_of[5], 1), 0, NODES - 1).astype(jnp.int32),
        "line_delay": place_ends(jax.random.randint(streams_of[6], (SUBNETS, LINES), STEPS, 2 * STEPS + 1), jax.random.fold_in(streams_of[6], 1), STEPS, 2 * STEPS).astype(jnp.int32),
        "line_admittance": jnp.clip(0.2 + 0.8 * jax.random.uniform(streams_of[7], (SUBNETS, LINES), jnp.float32) ** block_levels(streams_of[7], (SUBNETS, LINES), ((0, 256),), -0.2, 0.2), 0.2, 1.0),
        "conv_node": place_ends(jax.random.randint(streams_of[8], (SUBNETS, CONV), 0, NODES), jax.random.fold_in(streams_of[8], 1), 0, NODES - 1).astype(jnp.int32),
        "conv_count": draw_conv_count(jax.random.fold_in(streams_of[19], 71), 0),
        "conv_state": noise(streams_of[10], (SUBNETS, 2, CONV, CASES), 0.5, 3.0, ((0, 256),), jnp.float32),
        "conv_reference": noise(streams_of[11], (SUBNETS, 2, CONV, CASES), 1.0, 4.0, ((0, 256),), jnp.float32),
        "conv_rate": jnp.clip(jnp.exp(math.log(0.6) - 2.9957323 * jax.random.uniform(streams_of[12], (SUBNETS, CONV), jnp.float32) ** block_levels(streams_of[12], (SUBNETS, CONV), ((0, 256),), -0.2, 0.2)), 0.03, 0.6),
        "conv_limit": jnp.clip(1.0 + 1.5 * jax.random.uniform(streams_of[13], (SUBNETS, CONV), jnp.float32) ** block_levels(streams_of[13], (SUBNETS, CONV), ((0, 256),), -0.2, 0.2), 1.0, 2.5),
        "port_node": place_ends(jax.random.randint(streams_of[14], (SUBNETS, PORTS), 0, NODES), jax.random.fold_in(streams_of[14], 1), 0, NODES - 1).astype(jnp.int32),
        "port_admittance": jnp.clip(0.3 + 0.90000004 * jax.random.uniform(streams_of[15], (SUBNETS, PORTS), jnp.float32) ** block_levels(streams_of[15], (SUBNETS, PORTS), ((0, 256),), -0.2, 0.2), 0.3, 1.2),
        "port_voltage_prev": noise(streams_of[16], (2, SUBNETS, PORTS, CASES), 1.0, 5.0, ((1, 256),), jnp.float32),
        "port_bus": place_ends(jax.random.randint(streams_of[17], (SUBNETS, PORTS), 0, NB), jax.random.fold_in(streams_of[17], 1), 0, NB - 1).astype(jnp.int32),
        "transfer_impedance": noise(streams_of[18], (2, NB, NPORT), (NPORT // 4) ** -0.5, 0.25, ((1, 8), (2, 32)), jnp.float32),
    }


HIGHEST = lax.Precision.HIGHEST
SAG_FACTOR = 0.3


def window(ginv, start_hist, gcap, incoming, lnode, ladm, cnode, ccount, cstate, setpoint_flow, crate, climit, pnode, padm, pvolt):
    nodes = ginv.shape[0]
    lines = lnode.shape[0]
    convs = cnode.shape[0]
    index = jnp.concatenate([lnode, cnode, pnode]).astype(jnp.int32)
    onehot = (jnp.arange(nodes, dtype=jnp.int32)[:, None] == index[None, :]).astype(jnp.float32)
    picker = onehot.T
    live = (jnp.arange(convs, dtype=jnp.int32) < ccount)[:, None]
    angles = jnp.arange(1, STEPS + 1, dtype=jnp.float32) * jnp.float32(2.0 * math.pi / STEPS)
    limit = climit[:, None]
    slew_limit = crate[:, None]

    def advance(carry, inputs):
        hist_now, inverter_axial_part, inverter_normal_part, acc_re, acc_im = carry
        inward, angle = inputs
        angle_cos_factor = jnp.cos(angle)
        angle_sin_factor = jnp.sin(angle)
        drive = jnp.where(live, inverter_axial_part * angle_cos_factor - inverter_normal_part * angle_sin_factor, 0.0)
        source = padm[:, None] * (pvolt[0] * angle_cos_factor - pvolt[1] * angle_sin_factor)
        stacked = jnp.concatenate([inward, drive, source], axis=0)
        right = hist_now + jnp.dot(onehot, stacked, precision=HIGHEST)
        volt = jnp.dot(ginv, right, precision=HIGHEST)
        probe = jnp.dot(picker, volt, precision=HIGHEST)
        at_line = probe[:lines]
        inverter_emf = probe[lines:lines + convs]
        at_port = probe[lines + convs:]
        outward = 2.0 * ladm[:, None] * at_line - inward
        flow = source - padm[:, None] * at_port
        acc_re = acc_re + flow * angle_cos_factor
        acc_im = acc_im - flow * angle_sin_factor
        unclipped_axial_part = inverter_axial_part + slew_limit * (setpoint_flow[0] - inverter_axial_part) - SAG_FACTOR * inverter_emf * angle_cos_factor
        unclipped_normal_part = inverter_normal_part + slew_limit * (setpoint_flow[1] - inverter_normal_part) + SAG_FACTOR * inverter_emf * angle_sin_factor
        inverter_axial_part = jnp.where(live, limit * jnp.tanh(unclipped_axial_part / limit), inverter_axial_part)
        inverter_normal_part = jnp.where(live, limit * jnp.tanh(unclipped_normal_part / limit), inverter_normal_part)
        hist_now = 2.0 * gcap[:, None] * volt - hist_now
        return (hist_now, inverter_axial_part, inverter_normal_part, acc_re, acc_im), outward

    zeros = jnp.zeros(pvolt.shape[1:], dtype=jnp.float32)
    carry = (start_hist, cstate[0], cstate[1], zeros, zeros)
    carry, outward = lax.scan(advance, carry, (incoming, angles))
    hist_end, inverter_axial_part, inverter_normal_part, acc_re, acc_im = carry
    current = jnp.stack([acc_re, acc_im]) * jnp.float32(2.0 / STEPS)
    return outward, hist_end, jnp.stack([inverter_axial_part, inverter_normal_part]), current


def reference(conductance_inverse, cap_history, cap_conductance, wave_history, line_partner, line_node, line_delay, line_admittance, conv_node, conv_count, conv_state, conv_reference, conv_rate, conv_limit, port_node, port_admittance, port_voltage_prev, port_bus, transfer_impedance):
    remote = (jnp.arange(LINES, dtype=jnp.int32) + LINES // 2) % LINES
    times = jnp.arange(STEPS, dtype=jnp.int32)

    def one_subnet(items):
        ginv, start_hist, gcap, partner, lnode, delay, ladm, cnode, ccount, cstate, setpoint_flow, crate, climit, pnode, padm, pvolt = items
        rows = wave_history[partner, :, remote, :]
        where_now = (times[None, :] - delay[:, None] + HIST).astype(jnp.int32)
        delayed = jnp.take_along_axis(rows, where_now[:, :, None], axis=1)
        incoming = jnp.transpose(delayed, (1, 0, 2))
        return window(ginv, start_hist, gcap, incoming, lnode, ladm, cnode, ccount, cstate, setpoint_flow, crate, climit, pnode, padm, pvolt)

    pvolt_all = jnp.transpose(port_voltage_prev, (1, 0, 2, 3))
    waves, hist_end, conv_out, current = lax.map(one_subnet, (conductance_inverse, cap_history, cap_conductance, line_partner, line_node, line_delay, line_admittance, conv_node, conv_count, conv_state, conv_reference, conv_rate, conv_limit, port_node, port_admittance, pvolt_all))
    flat = jnp.transpose(current, (1, 0, 2, 3)).reshape(2, SUBNETS * PORTS, CASES)
    real = jnp.dot(transfer_impedance[0], flat[0], precision=HIGHEST) - jnp.dot(transfer_impedance[1], flat[1], precision=HIGHEST)
    imag = jnp.dot(transfer_impedance[0], flat[1], precision=HIGHEST) + jnp.dot(transfer_impedance[1], flat[0], precision=HIGHEST)
    bus_voltage = jnp.stack([real, imag])
    port_voltage = bus_voltage[:, port_bus.reshape(-1).astype(jnp.int32), :].reshape(2, SUBNETS, PORTS, CASES)
    return waves, hist_end, conv_out, bus_voltage, port_voltage
```

```python
import math

import jax
import jax.numpy as jnp
import numpy as np
from jax import lax
from jax.experimental import pallas as pl
from jax.experimental.pallas import tpu as pltpu
from jax.sharding import Mesh
from jax.sharding import PartitionSpec as P

STEPS = 20
HIST = 40
NEAR = 12
LINES = 32
CONV = 64
PORTS = 8
HALF = LINES // 2
PROBES = LINES + CONV + PORTS
SAG_FACTOR = 0.3
ALL = ("z", "x", "y", "core")
AREA = ("z", "x")
ROW = ("y", "core")
F32 = jnp.float32
BF16 = jnp.bfloat16

AT_DELAY = 128
AT_PARTNER = 160
AT_COUNT = 192


def dot(a, b):
    return jnp.dot(a, b, preferred_element_type=F32)


def split(x):
    high = x.astype(BF16)
    return high, (x - high.astype(F32)).astype(BF16)


def reach_of(table, line, base):
    return jnp.bitwise_and(table[base + line] - table[base + HALF + line], 255) // 2


def pack_kernel(partner, waves, near_up, far_up, near_down, far_down):
    near = jnp.int32(0)
    for line in range(HALF):
        is_near = reach_of(partner, line, 0) == 1
        up = waves[:, line, :]
        down = waves[:, line + HALF, :]

        @pl.when(is_near)
        def _(near=near, up=up, down=down):
            near_up[near] = up
            near_down[near] = down

        @pl.when(jnp.logical_not(is_near))
        def _(far=line - near, up=up, down=down):
            far_up[far] = up
            far_down[far] = down

        near = near + is_near.astype(jnp.int32)


def pack(partner, waves):
    hist, _, cases = waves.shape
    near = jax.ShapeDtypeStruct((NEAR, hist, cases), F32)
    far = jax.ShapeDtypeStruct((HALF - NEAR, hist, cases), F32)
    vmem = pl.BlockSpec(memory_space=pltpu.VMEM)
    return pl.pallas_call(
        pack_kernel,
        out_shape=(near, far, near, far),
        in_specs=[pl.BlockSpec(memory_space=pltpu.SMEM), vmem],
        out_specs=(vmem,) * 4,
        name="pack_waves",
    )(partner, waves)


def column(row):
    return jnp.broadcast_to(row, (128, 128)).T


def window_kernel(
    table,
    angle,
    g_hbm,
    hist0,
    near_up,
    far_up,
    near_down,
    far_down,
    nodes_row,
    gcap,
    line_row,
    rate_row,
    state0,
    setpoint,
    pvolt,
    waves,
    hist_out,
    state_out,
    current,
    g_in,
    g_high,
    g_low,
    arrived,
    incoming,
    w_even,
    w_odd,
    volt,
    probe,
    stack,
    cap2,
    coef,
    g_sem,
    a_sem,
):
    nodes = g_high.shape[0]
    chunks = g_in.shape[0]
    rows = nodes // chunks
    copies = [
        pltpu.make_async_copy(g_hbm.at[pl.ds(i * rows, rows)], g_in.at[i], g_sem.at[i])
        for i in range(chunks)
    ]
    for copy in copies:
        copy.start()
    first = 0
    moves = []
    for i, part in enumerate((near_up, far_up, near_down, far_down)):
        size = part.shape[0]
        moves.append(
            pltpu.make_async_copy(part, arrived.at[pl.ds(first, size)], a_sem.at[i])
        )
        first += size
    for move in moves:
        move.start()

    coef[0] = column(line_row[...])
    coef[1] = column(rate_row[...])
    for i in range(nodes // 128):
        cap2[pl.ds(i * 128, 128)] = 2.0 * column(gcap[:, pl.ds(i * 128, 128)])
    hist_out[...] = hist0[...]
    high, low = split(hist0[...])
    w_even[pl.ds(0, nodes), pl.ds(0, 128)] = high
    w_even[pl.ds(0, nodes), pl.ds(128, 128)] = low
    zeros = jnp.zeros((256, 128), BF16)
    for w in (w_even, w_odd):
        w[pl.ds(nodes, 256), pl.ds(0, 128)] = zeros
        w[pl.ds(nodes, 256), pl.ds(128, 128)] = zeros
    state_out[...] = state0[...]
    current[...] = jnp.zeros_like(current)
    stack[...] = jnp.zeros_like(stack)

    picks = (
        lax.broadcasted_iota(jnp.int32, (nodes, 128), 0) == nodes_row[...]
    ).astype(BF16)
    for i, copy in enumerate(copies):
        copy.wait()
        high, low = split(g_in[i])
        at = pl.ds(i * rows, rows)
        g_high[at, pl.ds(0, nodes)] = high
        g_low[at, :] = low
        g_high[at, pl.ds(nodes, 128)] = dot(high, picks).astype(BF16)
        g_high[at, pl.ds(nodes + 128, 128)] = dot(low, picks).astype(BF16)

    for move in moves:
        move.wait()
    near = jnp.int32(0)
    for line in range(HALF):
        is_near = reach_of(table, line, AT_PARTNER) == 1
        place = jnp.where(is_near, near, NEAR + line - near)
        near = near + is_near.astype(jnp.int32)
        for slot, at in ((line + HALF, place), (line, place + HALF)):
            start = HIST - table[AT_DELAY + slot]
            incoming[:, slot, :] = arrived[at, pl.ds(start, STEPS), :]

    line_adm = 2.0 * coef[0, :LINES]
    limit = coef[0, LINES : LINES + CONV]
    padm = coef[0, LINES + CONV : PROBES]
    rate = coef[1, LINES : LINES + CONV]
    inverse = 1.0 / limit
    live = lax.broadcasted_iota(jnp.int32, (CONV, 128), 0) < table[AT_COUNT]

    def step(t, w, w_next):
        cos, sin = angle[0, t], angle[1, t]
        axial, normal = state_out[0], state_out[1]
        inward = incoming[t]
        source = padm * (pvolt[0] * cos - pvolt[1] * sin)
        stack[pl.ds(0, LINES)] = inward
        stack[pl.ds(LINES, CONV)] = jnp.where(live, axial * cos - normal * sin, 0.0)
        stack[pl.ds(LINES + CONV, PORTS)] = source
        high, low = split(stack[...])
        w[pl.ds(nodes, 128), pl.ds(0, 128)] = high
        w[pl.ds(nodes, 128), pl.ds(128, 128)] = low
        w[pl.ds(nodes + 128, 128), pl.ds(0, 128)] = high
        block = 256
        for i in range(0, nodes, block):
            at = pl.ds(i, block)
            y = dot(g_high[at, :], w[...])
            z = dot(g_low[at, :], w[pl.ds(0, nodes), pl.ds(0, 128)])
            v = y[:, :128] + y[:, 128:] + z
            volt[at, :] = v
            h = cap2[at, :] * v - hist_out[at, :]
            hist_out[at, :] = h
            high, low = split(h)
            w_next[at, pl.ds(0, 128)] = high
            w_next[at, pl.ds(128, 128)] = low
        for k in range(PROBES):
            probe[pl.ds(k, 1), :] = volt[pl.ds(table[k], 1), :]
        emf = probe[pl.ds(LINES, CONV), :]
        new_axial = axial + rate * (setpoint[0] - axial) - (SAG_FACTOR * cos) * emf
        new_normal = normal + rate * (setpoint[1] - normal) + (SAG_FACTOR * sin) * emf
        state_out[0] = jnp.where(live, limit * jnp.tanh(new_axial * inverse), axial)
        state_out[1] = jnp.where(live, limit * jnp.tanh(new_normal * inverse), normal)
        waves[t] = line_adm * probe[pl.ds(0, LINES), :] - inward
        flow = source - padm * probe[pl.ds(LINES + CONV, PORTS), :]
        current[0] = current[0] + flow * cos
        current[1] = current[1] - flow * sin

    def pair(i, _):
        step(2 * i, w_even, w_odd)
        step(2 * i + 1, w_odd, w_even)
        return 0

    lax.fori_loop(0, STEPS // 2, pair, 0)
    current[...] = current[...] * (2.0 / STEPS)


def window(table, nodes_row, angle, ginv, hist0, arrivals, gcap, line_row, rate_row, state, setpoint, pvolt):
    nodes, cases = hist0.shape
    vmem = pl.BlockSpec(memory_space=pltpu.VMEM)
    smem = pl.BlockSpec(memory_space=pltpu.SMEM)
    far = pl.BlockSpec(memory_space=pl.ANY)
    chunks = 8
    return pl.pallas_call(
        window_kernel,
        out_shape=(
            jax.ShapeDtypeStruct((STEPS, LINES, cases), F32),
            jax.ShapeDtypeStruct((nodes, cases), F32),
            jax.ShapeDtypeStruct(state.shape, F32),
            jax.ShapeDtypeStruct((2, PORTS, cases), F32),
        ),
        in_specs=[smem, smem, far, vmem, far, far, far, far] + [vmem] * 7,
        out_specs=(vmem,) * 4,
        scratch_shapes=[
            pltpu.VMEM((chunks, nodes // chunks, nodes), F32),
            pltpu.VMEM((nodes, nodes + 256), BF16),
            pltpu.VMEM((nodes, nodes), BF16),
            pltpu.VMEM((LINES, HIST, cases), F32),
            pltpu.VMEM((STEPS, LINES, cases), F32),
            pltpu.VMEM((nodes + 256, 256), BF16),
            pltpu.VMEM((nodes + 256, 256), BF16),
            pltpu.VMEM((nodes, cases), F32),
            pltpu.VMEM((PROBES, cases), F32),
            pltpu.VMEM((128, cases), F32),
            pltpu.VMEM((nodes, cases), F32),
            pltpu.VMEM((2, 128, cases), F32),
            pltpu.SemaphoreType.DMA((chunks,)),
            pltpu.SemaphoreType.DMA((4,)),
        ],
        compiler_params=pltpu.CompilerParams(vmem_limit_bytes=40 << 20),
        cost_estimate=pl.CostEstimate(
            flops=6 * STEPS * nodes * nodes * cases,
            bytes_accessed=64 << 20,
            transcendentals=0,
        ),
        name="window",
    )(table, angle, ginv, hist0, *arrivals, nodes_row, gcap, line_row, rate_row, state, setpoint, pvolt)


def bus_kernel(impedance, current, out):
    members, areas = current.shape[:2]
    z = jnp.concatenate([impedance[i] for i in range(areas)], axis=1)
    parts = []
    for i in range(areas):
        real = jnp.concatenate([current[r, i, 0] for r in range(members)], axis=0)
        imag = jnp.concatenate([current[r, i, 1] for r in range(members)], axis=0)
        parts.append(jnp.concatenate([real, imag], axis=1))
        parts.append(jnp.concatenate([-imag, real], axis=1))
    w = jnp.concatenate(parts, axis=0)
    z_high, z_low = split(z)
    w_high, w_low = split(w)
    out[...] = dot(z_high, w_high) + dot(z_low, w_high) + dot(z_high, w_low)


def bus_product(impedance, current):
    vmem = pl.BlockSpec(memory_space=pltpu.VMEM)
    return pl.pallas_call(
        bus_kernel,
        out_shape=jax.ShapeDtypeStruct((impedance.shape[1], 256), F32),
        in_specs=[vmem] * 2,
        out_specs=vmem,
        compiler_params=pltpu.CompilerParams(vmem_limit_bytes=32 << 20),
        name="bus_product",
    )(impedance, current)


def port_kernel(local, volts, out, rows, sem):
    count = out.shape[0]
    most = volts.shape[0]

    def fetch(k):
        b = jnp.clip(local[k], 0, most - 1)
        start = pl.multiple_of((b // 8) * 8, 8)
        return pltpu.make_async_copy(volts.at[pl.ds(start, 8)], rows.at[k], sem.at[k])

    for k in range(count):
        fetch(k).start()
    for k in range(count):
        fetch(k).wait()
        b = local[k]
        here = jnp.logical_and(b >= 0, b < most)
        inside = jnp.bitwise_and(jnp.clip(b, 0, most - 1), 7)
        value = rows[k, pl.ds(inside, 1), :]
        out[pl.ds(k, 1), :] = jnp.where(here, value, 0.0)


def port_rows(local, volts):
    count = local.shape[0]
    width = volts.shape[1]
    return pl.pallas_call(
        port_kernel,
        out_shape=jax.ShapeDtypeStruct((count, width), F32),
        in_specs=[pl.BlockSpec(memory_space=pltpu.SMEM), pl.BlockSpec(memory_space=pl.ANY)],
        out_specs=pl.BlockSpec(memory_space=pltpu.VMEM),
        scratch_shapes=[pltpu.VMEM((count, 8, width), F32), pltpu.SemaphoreType.DMA((count,))],
        name="port_rows",
    )(local, volts)


def shifted(x, by):
    size = lax.axis_size(ALL)
    return lax.ppermute(x, ALL, [(i, (i + by) % size) for i in range(size)])


def copy_for_each(x, axis):
    size = lax.axis_size(axis)
    return lax.all_to_all(jnp.broadcast_to(x[None], (size, *x.shape)), axis, 0, 0, tiled=True)


def per_device(
    conductance_inverse,
    cap_history,
    cap_conductance,
    wave_history,
    line_partner,
    line_node,
    line_delay,
    line_admittance,
    conv_node,
    conv_count,
    conv_state,
    conv_reference,
    conv_rate,
    conv_limit,
    port_node,
    port_admittance,
    port_voltage_prev,
    port_bus,
    transfer_impedance,
):
    areas = lax.axis_size("z")
    bus_rows = transfer_impedance.shape[1]
    with jax.named_scope("wave_exchange"):
        near_up, far_up, near_down, far_down = pack(line_partner[0], wave_history[0])
        arrivals = (
            shifted(near_up, 1),
            shifted(far_up, 2),
            shifted(near_down, -1),
            shifted(far_down, -2),
        )
    with jax.named_scope("impedance_exchange"):
        both = jnp.concatenate([transfer_impedance[0], transfer_impedance[1]], axis=1)
        both = both.reshape(areas, bus_rows // areas, both.shape[1])
        impedance = lax.all_to_all(both, "z", 0, 0, tiled=True)
    with jax.named_scope("tables"):
        spare = jnp.full((128 - PROBES,), -1, jnp.int32)
        nodes = jnp.concatenate([line_node[0], conv_node[0], port_node[0], spare])
        rest = jnp.zeros((256 - AT_COUNT - 1,), jnp.int32)
        table = jnp.concatenate([nodes, line_delay[0], line_partner[0], conv_count, rest])
        gap = jnp.ones((128 - PROBES,), F32)
        line_row = jnp.concatenate([line_admittance[0], conv_limit[0], port_admittance[0], gap])
        rate_row = jnp.concatenate(
            [jnp.zeros((LINES,), F32), conv_rate[0], jnp.zeros((128 - LINES - CONV,), F32)]
        )
        theta = np.arange(1, STEPS + 1, dtype=np.float32) * np.float32(2.0 * math.pi / STEPS)
        angle = jnp.asarray(np.stack([np.cos(theta), np.sin(theta)]).astype(np.float32))
    outward, hist_end, conv_out, current = window(
        table,
        nodes[None],
        angle,
        conductance_inverse[0],
        cap_history[0],
        arrivals,
        cap_conductance,
        line_row[None],
        rate_row[None],
        conv_state[0],
        conv_reference[0],
        port_voltage_prev[:, 0],
    )
    with jax.named_scope("currents"):
        flat = copy_for_each(copy_for_each(current, "z"), ROW)
        flat = flat.reshape(lax.axis_size(ROW), areas, *current.shape)
    with jax.named_scope("bus_voltage"):
        partial = bus_product(impedance, flat)
        size = lax.axis_size("x")
        pieces = partial.reshape(size, -1, partial.shape[1])
        own = jnp.sum(lax.all_to_all(pieces, "x", 0, 0, tiled=True), axis=0)
        volts = copy_for_each(own, "x")
        volts = lax.all_gather(volts.reshape(-1, volts.shape[-1]), "z", tiled=True)
        cases = volts.shape[1] // 2
        bus_voltage = jnp.stack([volts[:, :cases], volts[:, cases:]])
    with jax.named_scope("port_voltage"):
        local = port_bus.reshape(-1) - lax.axis_index(ROW) * bus_rows
        picked = port_rows(local, volts)
        members = port_bus.shape[0]
        picked = picked.reshape(members, PORTS, 2 * cases)
        mine = jnp.sum(lax.all_to_all(picked, ROW, 0, 0, tiled=True), axis=0)
        port_voltage = jnp.stack([mine[:, :cases], mine[:, cases:]])[:, None]
    return (outward[None], hist_end[None], conv_out[None], bus_voltage, port_voltage)


def solution(mesh):
    devices = mesh.devices.reshape(8, 4, 4, 2)
    torus = Mesh(devices, ALL)
    return jax.shard_map(
        per_device,
        mesh=torus,
        in_specs=(
            P(ALL, None, None),
            P(ALL, None, None),
            P(ALL, None),
            P(ALL, None, None, None),
            P(ALL, None),
            P(ALL, None),
            P(ALL, None),
            P(ALL, None),
            P(ALL, None),
            P(ALL),
            P(ALL, None, None, None),
            P(ALL, None, None, None),
            P(ALL, None),
            P(ALL, None),
            P(ALL, None),
            P(ALL, None),
            P(None, ALL, None, None),
            P(AREA, None),
            P(None, ROW, AREA),
        ),
        out_specs=(
            P(ALL, None, None, None),
            P(ALL, None, None),
            P(ALL, None, None, None),
            P(None, ROW, None),
            P(None, ALL, None, None),
        ),
        check_vma=False,
    )
```

```python
import math

import jax
import jax.numpy as jnp
import numpy as np
from jax import lax
from jax.experimental import pallas as pl
from jax.experimental.pallas import tpu as pltpu
from jax.sharding import Mesh
from jax.sharding import PartitionSpec as P

STEPS = 20
HIST = 40
NEAR = 12
LINES = 32
CONV = 64
PORTS = 8
HALF = LINES // 2
PROBES = LINES + CONV + PORTS
SAG_FACTOR = 0.3
ALL = ("z", "x", "y", "core")
AREA = ("z", "x")
ROW = ("y", "core")
F32 = jnp.float32
BF16 = jnp.bfloat16


def dot(a, b):
    return jnp.dot(a, b, preferred_element_type=F32)


def split(x):
    high = x.astype(BF16)
    return high, (x - high.astype(F32)).astype(BF16)


def reach_of(partner, line):
    return jnp.bitwise_and(partner[0, line] - partner[0, HALF + line], 255) // 2


def pack_kernel(partner, waves, impedance, ports, near_up, far_up, near_down, far_down, blocks):
    near = jnp.int32(0)
    for line in range(HALF):
        is_near = reach_of(partner, line) == 1
        up = waves[:, line, :]
        down = waves[:, line + HALF, :]

        @pl.when(is_near)
        def _(near=near, up=up, down=down):
            near_up[near] = up
            near_down[near] = down

        @pl.when(jnp.logical_not(is_near))
        def _(far=line - near, up=up, down=down):
            far_up[far] = up
            far_down[far] = down

        near = near + is_near.astype(jnp.int32)
    areas, rows, _ = blocks.shape
    rows = rows - 8
    for first in range(0, areas * rows, 128):
        part = impedance[:, :, pl.ds(first, 128)]
        turned = jnp.concatenate([part[0], part[1]], axis=0).T
        done = 0
        while done < 128:
            area, at = divmod(first + done, rows)
            size = min(128 - done, rows - at)
            blocks[area, pl.ds(at, size), :] = turned[done : done + size]
            done += size
    for area in range(areas):
        blocks[area, pl.ds(rows, 8), :] = jnp.broadcast_to(ports[...], (8, 128))


def pack(partner, waves, impedance, ports, areas):
    hist, _, cases = waves.shape
    near = jax.ShapeDtypeStruct((NEAR, hist, cases), F32)
    far = jax.ShapeDtypeStruct((HALF - NEAR, hist, cases), F32)
    blocks = jax.ShapeDtypeStruct((areas, impedance.shape[2] // areas + 8, 128), F32)
    vmem = pl.BlockSpec(memory_space=pltpu.VMEM)
    return pl.pallas_call(
        pack_kernel,
        out_shape=(near, far, near, far, blocks),
        in_specs=[pl.BlockSpec(memory_space=pltpu.SMEM), vmem, vmem, vmem],
        out_specs=(vmem,) * 5,
        compiler_params=pltpu.CompilerParams(vmem_limit_bytes=32 << 20),
        name="pack_waves",
    )(partner, waves, impedance, ports)


def column(row):
    return jnp.broadcast_to(row, (128, 128)).T


def window_kernel(
    angle,
    partner,
    delay,
    count,
    line_node,
    conv_node,
    port_node,
    g_hbm,
    hist0_hbm,
    gcap_hbm,
    state0_hbm,
    setpoint_hbm,
    pvolt_hbm,
    near_up,
    far_up,
    near_down,
    far_down,
    line_nodes,
    conv_nodes,
    port_nodes,
    line_adms,
    limits,
    rates,
    port_adms,
    waves,
    hist_out,
    state_out,
    current,
    g_in,
    g_high,
    g_low,
    arrived,
    incoming,
    w_even,
    w_odd,
    volt,
    probe,
    stack,
    cap2,
    coef,
    setpoint,
    pvolt,
    gcap,
    nodes_row,
    coef_row,
    g_sem,
    a_sem,
    s_sem,
):
    nodes = g_high.shape[0]
    chunks = g_in.shape[0]
    rows = nodes // chunks
    small = []

    def bring(source, target):
        small.append(pltpu.make_async_copy(source, target, s_sem.at[len(small)]))
        small[-1].start()

    bring(gcap_hbm, gcap)
    bring(hist0_hbm, hist_out)
    bring(state0_hbm, state_out)
    bring(setpoint_hbm, setpoint)
    bring(pvolt_hbm, pvolt)
    copies = [
        pltpu.make_async_copy(g_hbm.at[pl.ds(i * rows, rows)], g_in.at[i], g_sem.at[i])
        for i in range(chunks)
    ]
    for copy in copies:
        copy.start()
    first = 0
    moves = []
    for i, part in enumerate((near_up, far_up, near_down, far_down)):
        size = part.shape[0]
        moves.append(
            pltpu.make_async_copy(part, arrived.at[pl.ds(first, size)], a_sem.at[i])
        )
        first += size
    for move in moves:
        move.start()

    zeros = jnp.zeros((256, 128), BF16)
    for w in (w_even, w_odd):
        w[pl.ds(nodes, 256), pl.ds(0, 128)] = zeros
        w[pl.ds(nodes, 256), pl.ds(128, 128)] = zeros
    current[...] = jnp.zeros_like(current)
    stack[...] = jnp.zeros_like(stack)
    nodes_row[...] = jnp.full(nodes_row.shape, -1, jnp.int32)
    coef_row[...] = jnp.ones(coef_row.shape, F32)
    for copy in small:
        copy.wait()

    at_conv, at_port = pl.ds(LINES, CONV), pl.ds(LINES + CONV, PORTS)
    first_row = pl.ds(0, 1)
    nodes_row[first_row, pl.ds(0, LINES)] = line_nodes[...]
    nodes_row[first_row, at_conv] = conv_nodes[...]
    nodes_row[first_row, at_port] = port_nodes[...]
    coef_row[first_row, pl.ds(0, LINES)] = line_adms[...]
    coef_row[first_row, at_conv] = limits[...]
    coef_row[first_row, at_port] = port_adms[...]
    coef_row[pl.ds(1, 1), at_conv] = rates[...]
    coef[0] = column(coef_row[pl.ds(0, 1), :])
    coef[1] = column(coef_row[pl.ds(1, 1), :])
    for i in range(nodes // 128):
        cap2[pl.ds(i * 128, 128)] = 2.0 * column(gcap[:, pl.ds(i * 128, 128)])
    high, low = split(hist_out[...])
    w_even[pl.ds(0, nodes), pl.ds(0, 128)] = high
    w_even[pl.ds(0, nodes), pl.ds(128, 128)] = low

    picks = (
        lax.broadcasted_iota(jnp.int32, (nodes, 128), 0) == nodes_row[pl.ds(0, 1), :]
    ).astype(BF16)
    for i, copy in enumerate(copies):
        copy.wait()
        high, low = split(g_in[i])
        at = pl.ds(i * rows, rows)
        g_high[at, pl.ds(0, nodes)] = high
        g_low[at, :] = low
        g_high[at, pl.ds(nodes, 128)] = dot(high, picks).astype(BF16)
        g_high[at, pl.ds(nodes + 128, 128)] = dot(low, picks).astype(BF16)

    for move in moves:
        move.wait()
    near = jnp.int32(0)
    for line in range(HALF):
        is_near = reach_of(partner, line) == 1
        place = jnp.where(is_near, near, NEAR + line - near)
        near = near + is_near.astype(jnp.int32)
        for slot, at in ((line + HALF, place), (line, place + HALF)):
            start = HIST - delay[0, slot]
            incoming[:, slot, :] = arrived[at, pl.ds(start, STEPS), :]

    line_adm = 2.0 * coef[0, :LINES]
    limit = coef[0, LINES : LINES + CONV]
    padm = coef[0, LINES + CONV : PROBES]
    rate = coef[1, LINES : LINES + CONV]
    inverse = 1.0 / limit
    live = lax.broadcasted_iota(jnp.int32, (CONV, 128), 0) < count[0]

    def step(t, w, w_next):
        cos, sin = angle[0, t], angle[1, t]
        axial, normal = state_out[0], state_out[1]
        inward = incoming[t]
        source = padm * (pvolt[0] * cos - pvolt[1] * sin)
        stack[pl.ds(0, LINES)] = inward
        stack[pl.ds(LINES, CONV)] = jnp.where(live, axial * cos - normal * sin, 0.0)
        stack[pl.ds(LINES + CONV, PORTS)] = source
        high, low = split(stack[...])
        w[pl.ds(nodes, 128), pl.ds(0, 128)] = high
        w[pl.ds(nodes, 128), pl.ds(128, 128)] = low
        w[pl.ds(nodes + 128, 128), pl.ds(0, 128)] = high
        block = 256
        for i in range(0, nodes, block):
            at = pl.ds(i, block)
            y = dot(g_high[at, :], w[...])
            z = dot(g_low[at, :], w[pl.ds(0, nodes), pl.ds(0, 128)])
            v = y[:, :128] + y[:, 128:] + z
            volt[at, :] = v
            h = cap2[at, :] * v - hist_out[at, :]
            hist_out[at, :] = h
            high, low = split(h)
            w_next[at, pl.ds(0, 128)] = high
            w_next[at, pl.ds(128, 128)] = low
        for base, where in ((0, line_node), (LINES, conv_node), (LINES + CONV, port_node)):
            for k in range(where.shape[1]):
                probe[pl.ds(base + k, 1), :] = volt[pl.ds(where[0, k], 1), :]
        emf = probe[pl.ds(LINES, CONV), :]
        new_axial = axial + rate * (setpoint[0] - axial) - (SAG_FACTOR * cos) * emf
        new_normal = normal + rate * (setpoint[1] - normal) + (SAG_FACTOR * sin) * emf
        state_out[0] = jnp.where(live, limit * jnp.tanh(new_axial * inverse), axial)
        state_out[1] = jnp.where(live, limit * jnp.tanh(new_normal * inverse), normal)
        waves[t] = line_adm * probe[pl.ds(0, LINES), :] - inward
        flow = source - padm * probe[pl.ds(LINES + CONV, PORTS), :]
        current[0] = current[0] + flow * cos
        current[1] = current[1] - flow * sin

    def pair(i, _):
        step(2 * i, w_even, w_odd)
        step(2 * i + 1, w_odd, w_even)
        return 0

    lax.fori_loop(0, STEPS // 2, pair, 0)
    current[...] = current[...] * (2.0 / STEPS)


def window(angle, whole_numbers, ginv, hist0, arrivals, gcap, state, setpoint, pvolt, nodes_of, coefficients):
    nodes, cases = hist0.shape
    smem = pl.BlockSpec(memory_space=pltpu.SMEM)
    vmem = pl.BlockSpec(memory_space=pltpu.VMEM)
    chunks = 8
    scalars = (angle, *whole_numbers, *nodes_of)
    far = (ginv, hist0, gcap, state, setpoint, pvolt)
    rows = (*arrivals, *nodes_of, *coefficients)
    return pl.pallas_call(
        window_kernel,
        out_shape=(
            jax.ShapeDtypeStruct((STEPS, LINES, cases), F32),
            jax.ShapeDtypeStruct((nodes, cases), F32),
            jax.ShapeDtypeStruct(state.shape, F32),
            jax.ShapeDtypeStruct((2, PORTS, cases), F32),
        ),
        in_specs=[smem] * len(scalars)
        + [pl.BlockSpec(memory_space=pl.ANY)] * len(far)
        + [vmem] * len(rows),
        out_specs=(vmem,) * 4,
        scratch_shapes=[
            pltpu.VMEM((chunks, nodes // chunks, nodes), F32),
            pltpu.VMEM((nodes, nodes + 256), BF16),
            pltpu.VMEM((nodes, nodes), BF16),
            pltpu.VMEM((LINES, HIST, cases), F32),
            pltpu.VMEM((STEPS, LINES, cases), F32),
            pltpu.VMEM((nodes + 256, 256), BF16),
            pltpu.VMEM((nodes + 256, 256), BF16),
            pltpu.VMEM((nodes, cases), F32),
            pltpu.VMEM((PROBES, cases), F32),
            pltpu.VMEM((128, cases), F32),
            pltpu.VMEM((nodes, cases), F32),
            pltpu.VMEM((2, 128, cases), F32),
            pltpu.VMEM(setpoint.shape, F32),
            pltpu.VMEM(pvolt.shape, F32),
            pltpu.VMEM(gcap.shape, F32),
            pltpu.VMEM((8, 128), jnp.int32),
            pltpu.VMEM((8, 128), F32),
            pltpu.SemaphoreType.DMA((chunks,)),
            pltpu.SemaphoreType.DMA((4,)),
            pltpu.SemaphoreType.DMA((5,)),
        ],
        compiler_params=pltpu.CompilerParams(vmem_limit_bytes=44 << 20),
        cost_estimate=pl.CostEstimate(
            flops=6 * STEPS * nodes * nodes * cases,
            bytes_accessed=64 << 20,
            transcendentals=0,
        ),
        name="window",
    )(*scalars, *far, *rows)


def spread_kernel(current, impedance, out):
    for i in range(out.shape[0]):
        out[i] = current[...]


def spread(current, impedance, size):
    vmem = pl.BlockSpec(memory_space=pltpu.VMEM)
    return pl.pallas_call(
        spread_kernel,
        out_shape=jax.ShapeDtypeStruct((size, *current.shape), F32),
        in_specs=[vmem, pl.BlockSpec(memory_space=pl.ANY)],
        out_specs=vmem,
        compiler_params=pltpu.CompilerParams(vmem_limit_bytes=16 << 20),
        name="spread_currents",
    )(current, impedance)


def bus_kernel(impedance, current, out):
    areas, members = current.shape[:2]
    rows = pl.ds(0, out.shape[0])
    z = jnp.concatenate([impedance[i, rows, :] for i in range(areas)], axis=1)
    parts = []
    for i in range(areas):
        real = jnp.concatenate([current[i, r, 0] for r in range(members)], axis=0)
        imag = jnp.concatenate([current[i, r, 1] for r in range(members)], axis=0)
        parts.append(jnp.concatenate([real, imag], axis=1))
        parts.append(jnp.concatenate([-imag, real], axis=1))
    w = jnp.concatenate(parts, axis=0)
    z_high, z_low = split(z)
    w_high, w_low = split(w)
    out[...] = dot(z_high, w_high) + dot(z_low, w_high) + dot(z_high, w_low)


def bus_product(impedance, current):
    vmem = pl.BlockSpec(memory_space=pltpu.VMEM)
    return pl.pallas_call(
        bus_kernel,
        out_shape=jax.ShapeDtypeStruct((impedance.shape[1] - 8, 256), F32),
        in_specs=[vmem] * 2,
        out_specs=vmem,
        compiler_params=pltpu.CompilerParams(vmem_limit_bytes=32 << 20),
        name="bus_product",
    )(impedance, current)


def port_kernel(first, ports, volts, out):
    rows = volts.shape[0]
    high, rest = split(volts[...])
    middle = volts[...] - high.astype(F32)
    low = (middle - rest.astype(F32)).astype(BF16)
    row = lax.broadcasted_iota(jnp.int32, (rows, 128), 0) + first[0]
    for area in range(ports.shape[0]):
        wanted = ports[area, pl.ds(rows, 1), :].astype(jnp.int32)
        picks = jnp.where(row == wanted, 1.0, 0.0).T.astype(BF16)
        found = dot(picks, high) + dot(picks, rest) + dot(picks, low)
        count = out.shape[1] * out.shape[2]
        out[area] = found[:count].reshape(out.shape[1:])


def port_rows(first, ports, volts, members):
    vmem = pl.BlockSpec(memory_space=pltpu.VMEM)
    return pl.pallas_call(
        port_kernel,
        out_shape=jax.ShapeDtypeStruct((ports.shape[0], members, PORTS, volts.shape[1]), F32),
        in_specs=[pl.BlockSpec(memory_space=pltpu.SMEM), vmem, vmem],
        out_specs=vmem,
        compiler_params=pltpu.CompilerParams(vmem_limit_bytes=32 << 20),
        name="port_rows",
    )(first, ports, volts)


def shifted(x, by):
    size = lax.axis_size(ALL)
    return lax.ppermute(x, ALL, [(i, (i + by) % size) for i in range(size)])


def copy_for_each(x, axis):
    size = lax.axis_size(axis)
    return lax.all_to_all(jnp.broadcast_to(x[None], (size, *x.shape)), axis, 0, 0, tiled=True)


def per_device(
    conductance_inverse,
    cap_history,
    cap_conductance,
    wave_history,
    line_partner,
    line_node,
    line_delay,
    line_admittance,
    conv_node,
    conv_count,
    conv_state,
    conv_reference,
    conv_rate,
    conv_limit,
    port_node,
    port_admittance,
    port_voltage_prev,
    port_bus,
    transfer_impedance,
):
    areas = lax.axis_size("z")
    members = lax.axis_size(ROW)
    bus_rows = transfer_impedance.shape[1]
    with jax.named_scope("wave_exchange"):
        ports = port_bus.reshape(1, -1).astype(F32)
        ports = jnp.pad(ports, ((0, 0), (0, 128 - ports.shape[1])), constant_values=-1.0)
        turned = jnp.swapaxes(transfer_impedance, 1, 2)
        near_up, far_up, near_down, far_down, blocks = pack(
            line_partner, wave_history[0], turned, ports, areas
        )
        arrivals = (
            shifted(near_up, 1),
            shifted(far_up, 2),
            shifted(near_down, -1),
            shifted(far_down, -2),
        )
    with jax.named_scope("impedance_exchange"):
        impedance = lax.all_to_all(blocks, "z", 0, 0, tiled=True)
    with jax.named_scope("window"):
        theta = np.arange(1, STEPS + 1, dtype=np.float32) * np.float32(2.0 * math.pi / STEPS)
        angle = jnp.asarray(np.stack([np.cos(theta), np.sin(theta)]).astype(np.float32))
        outward, hist_end, conv_out, current = window(
            angle,
            (line_partner, line_delay, conv_count),
            conductance_inverse[0],
            cap_history[0],
            arrivals,
            cap_conductance,
            conv_state[0],
            conv_reference[0],
            port_voltage_prev[:, 0],
            (line_node, conv_node, port_node),
            (line_admittance, conv_limit, conv_rate, port_admittance),
        )
    with jax.named_scope("currents"):
        flat = spread(current, impedance, areas * members)
        flat = lax.all_to_all(flat, ("z", *ROW), 0, 0, tiled=True)
        flat = flat.reshape(areas, members, *current.shape)
    with jax.named_scope("bus_voltage"):
        partial = bus_product(impedance, flat)
        size = lax.axis_size("x")
        pieces = partial.reshape(size, -1, partial.shape[1])
        own = jnp.sum(lax.all_to_all(pieces, "x", 0, 0, tiled=True), axis=0)
        block = copy_for_each(own, "x").reshape(partial.shape)
        volts = lax.all_gather(block, "z", tiled=True)
        cases = volts.shape[1] // 2
        bus_voltage = jnp.stack([volts[:, :cases], volts[:, cases:]])
    with jax.named_scope("port_voltage"):
        first = lax.axis_index(ROW) * bus_rows + lax.axis_index("z") * partial.shape[0]
        picked = port_rows(first[None].astype(jnp.int32), impedance, block, members)
        picked = picked.reshape(areas * members, PORTS, 2 * cases)
        mine = jnp.sum(lax.all_to_all(picked, ("z", *ROW), 0, 0, tiled=True), axis=0)
        port_voltage = jnp.stack([mine[:, :cases], mine[:, cases:]])[:, None]
    return (outward[None], hist_end[None], conv_out[None], bus_voltage, port_voltage)


def solution(mesh):
    devices = mesh.devices.reshape(8, 4, 4, 2)
    torus = Mesh(devices, ALL)
    return jax.shard_map(
        per_device,
        mesh=torus,
        in_specs=(
            P(ALL, None, None),
            P(ALL, None, None),
            P(ALL, None),
            P(ALL, None, None, None),
            P(ALL, None),
            P(ALL, None),
            P(ALL, None),
            P(ALL, None),
            P(ALL, None),
            P(ALL),
            P(ALL, None, None, None),
            P(ALL, None, None, None),
            P(ALL, None),
            P(ALL, None),
            P(ALL, None),
            P(ALL, None),
            P(None, ALL, None, None),
            P(AREA, None),
            P(None, ROW, AREA),
        ),
        out_specs=(
            P(ALL, None, None, None),
            P(ALL, None, None),
            P(ALL, None, None, None),
            P(None, ROW, None),
            P(None, ALL, None, None),
        ),
        check_vma=False,
    )
```

```python
import math

import jax
import jax.numpy as jnp
import numpy as np
from jax import lax
from jax.experimental import pallas as pl
from jax.experimental.pallas import tpu as pltpu
from jax.sharding import Mesh
from jax.sharding import PartitionSpec as P

STEPS = 20
HIST = 40
NEAR = 12
LINES = 32
CONV = 64
PORTS = 8
HALF = LINES // 2
PROBES = LINES + CONV + PORTS
SAG_FACTOR = 0.3
ALL = ("z", "x", "y", "core")
AREA = ("z", "x")
ROW = ("y", "core")
F32 = jnp.float32
BF16 = jnp.bfloat16


def dot(a, b):
    return jnp.dot(a, b, preferred_element_type=F32)


def split(x):
    high = x.astype(BF16)
    return high, (x - high.astype(F32)).astype(BF16)


def reach_of(partner, line):
    return jnp.bitwise_and(partner[0, line] - partner[0, HALF + line], 255) // 2


def pack_kernel(partner, waves, near_up, far_up, near_down, far_down):
    near = jnp.int32(0)
    for line in range(HALF):
        is_near = reach_of(partner, line) == 1
        up = waves[:, line, :]
        down = waves[:, line + HALF, :]

        @pl.when(is_near)
        def _(near=near, up=up, down=down):
            near_up[near] = up
            near_down[near] = down

        @pl.when(jnp.logical_not(is_near))
        def _(far=line - near, up=up, down=down):
            far_up[far] = up
            far_down[far] = down

        near = near + is_near.astype(jnp.int32)


def pack(partner, waves):
    hist, _, cases = waves.shape
    near = jax.ShapeDtypeStruct((NEAR, hist, cases), F32)
    far = jax.ShapeDtypeStruct((HALF - NEAR, hist, cases), F32)
    vmem = pl.BlockSpec(memory_space=pltpu.VMEM)
    return pl.pallas_call(
        pack_kernel,
        out_shape=(near, far, near, far),
        in_specs=[pl.BlockSpec(memory_space=pltpu.SMEM), vmem],
        out_specs=(vmem,) * 4,
        compiler_params=pltpu.CompilerParams(vmem_limit_bytes=32 << 20),
        name="pack_waves",
    )(partner, waves)


def turn_kernel(impedance, ports, *rest):
    blocks = rest[-1]
    areas, rows, _ = blocks.shape
    rows = rows - 8
    for first in range(0, areas * rows, 128):
        part = impedance[:, :, pl.ds(first, 128)]
        turned = jnp.concatenate([part[0], part[1]], axis=0).T
        done = 0
        while done < 128:
            area, at = divmod(first + done, rows)
            size = min(128 - done, rows - at)
            blocks[area, pl.ds(at, size), :] = turned[done : done + size]
            done += size
    for area in range(areas):
        blocks[area, pl.ds(rows, 8), :] = jnp.broadcast_to(ports[...], (8, 128))


def turn(impedance, ports, arrivals, areas):
    vmem = pl.BlockSpec(memory_space=pltpu.VMEM)
    return pl.pallas_call(
        turn_kernel,
        out_shape=jax.ShapeDtypeStruct((areas, impedance.shape[2] // areas + 8, 128), F32),
        in_specs=[vmem] * (2 + len(arrivals)),
        out_specs=vmem,
        compiler_params=pltpu.CompilerParams(vmem_limit_bytes=32 << 20),
        name="turn_impedance",
    )(impedance, ports, *arrivals)


def column(row):
    return jnp.broadcast_to(row, (128, 128)).T


def window_kernel(
    angle,
    partner,
    delay,
    count,
    line_node,
    conv_node,
    port_node,
    g_hbm,
    hist0_hbm,
    gcap_hbm,
    state0_hbm,
    setpoint_hbm,
    pvolt_hbm,
    near_up,
    far_up,
    near_down,
    far_down,
    line_nodes,
    conv_nodes,
    port_nodes,
    line_adms,
    limits,
    rates,
    port_adms,
    waves,
    hist_out,
    state_out,
    current,
    g_in,
    g_high,
    g_low,
    arrived,
    incoming,
    w_even,
    w_odd,
    volt,
    probe,
    stack,
    cap2,
    coef,
    setpoint,
    pvolt,
    gcap,
    nodes_row,
    coef_row,
    g_sem,
    a_sem,
    s_sem,
):
    nodes = g_high.shape[0]
    chunks = g_in.shape[0]
    rows = nodes // chunks
    small = []

    def bring(source, target):
        small.append(pltpu.make_async_copy(source, target, s_sem.at[len(small)]))
        small[-1].start()

    bring(gcap_hbm, gcap)
    bring(hist0_hbm, hist_out)
    bring(state0_hbm, state_out)
    bring(setpoint_hbm, setpoint)
    bring(pvolt_hbm, pvolt)
    copies = [
        pltpu.make_async_copy(g_hbm.at[pl.ds(i * rows, rows)], g_in.at[i], g_sem.at[i])
        for i in range(chunks)
    ]
    for copy in copies:
        copy.start()
    first = 0
    moves = []
    for i, part in enumerate((near_up, far_up, near_down, far_down)):
        size = part.shape[0]
        moves.append(
            pltpu.make_async_copy(part, arrived.at[pl.ds(first, size)], a_sem.at[i])
        )
        first += size
    for move in moves:
        move.start()

    zeros = jnp.zeros((256, 128), BF16)
    for w in (w_even, w_odd):
        w[pl.ds(nodes, 256), pl.ds(0, 128)] = zeros
        w[pl.ds(nodes, 256), pl.ds(128, 128)] = zeros
    current[...] = jnp.zeros_like(current)
    stack[...] = jnp.zeros_like(stack)
    nodes_row[...] = jnp.full(nodes_row.shape, -1, jnp.int32)
    coef_row[...] = jnp.ones(coef_row.shape, F32)
    for copy in small:
        copy.wait()

    at_conv, at_port = pl.ds(LINES, CONV), pl.ds(LINES + CONV, PORTS)
    first_row = pl.ds(0, 1)
    nodes_row[first_row, pl.ds(0, LINES)] = line_nodes[...]
    nodes_row[first_row, at_conv] = conv_nodes[...]
    nodes_row[first_row, at_port] = port_nodes[...]
    coef_row[first_row, pl.ds(0, LINES)] = line_adms[...]
    coef_row[first_row, at_conv] = limits[...]
    coef_row[first_row, at_port] = port_adms[...]
    coef_row[pl.ds(1, 1), at_conv] = rates[...]
    coef[0] = column(coef_row[pl.ds(0, 1), :])
    coef[1] = column(coef_row[pl.ds(1, 1), :])
    for i in range(nodes // 128):
        cap2[pl.ds(i * 128, 128)] = 2.0 * column(gcap[:, pl.ds(i * 128, 128)])
    high, low = split(hist_out[...])
    w_even[pl.ds(0, nodes), pl.ds(0, 128)] = high
    w_even[pl.ds(0, nodes), pl.ds(128, 128)] = low

    picks = (
        lax.broadcasted_iota(jnp.int32, (nodes, 128), 0) == nodes_row[pl.ds(0, 1), :]
    ).astype(BF16)
    for i, copy in enumerate(copies):
        copy.wait()
        high, low = split(g_in[i])
        at = pl.ds(i * rows, rows)
        g_high[at, pl.ds(0, nodes)] = high
        g_low[at, :] = low
        g_high[at, pl.ds(nodes, 128)] = dot(high, picks).astype(BF16)
        g_high[at, pl.ds(nodes + 128, 128)] = dot(low, picks).astype(BF16)

    for move in moves:
        move.wait()
    near = jnp.int32(0)
    for line in range(HALF):
        is_near = reach_of(partner, line) == 1
        place = jnp.where(is_near, near, NEAR + line - near)
        near = near + is_near.astype(jnp.int32)
        for slot, at in ((line + HALF, place), (line, place + HALF)):
            start = HIST - delay[0, slot]
            incoming[:, slot, :] = arrived[at, pl.ds(start, STEPS), :]

    line_adm = 2.0 * coef[0, :LINES]
    limit = coef[0, LINES : LINES + CONV]
    padm = coef[0, LINES + CONV : PROBES]
    rate = coef[1, LINES : LINES + CONV]
    inverse = 1.0 / limit
    live = lax.broadcasted_iota(jnp.int32, (CONV, 128), 0) < count[0]

    def step(t, w, w_next):
        cos, sin = angle[0, t], angle[1, t]
        axial, normal = state_out[0], state_out[1]
        inward = incoming[t]
        source = padm * (pvolt[0] * cos - pvolt[1] * sin)
        stack[pl.ds(0, LINES)] = inward
        stack[pl.ds(LINES, CONV)] = jnp.where(live, axial * cos - normal * sin, 0.0)
        stack[pl.ds(LINES + CONV, PORTS)] = source
        high, low = split(stack[...])
        w[pl.ds(nodes, 128), pl.ds(0, 128)] = high
        w[pl.ds(nodes, 128), pl.ds(128, 128)] = low
        w[pl.ds(nodes + 128, 128), pl.ds(0, 128)] = high
        block = 256
        for i in range(0, nodes, block):
            at = pl.ds(i, block)
            y = dot(g_high[at, :], w[...])
            z = dot(g_low[at, :], w[pl.ds(0, nodes), pl.ds(0, 128)])
            v = y[:, :128] + y[:, 128:] + z
            volt[at, :] = v
            h = cap2[at, :] * v - hist_out[at, :]
            hist_out[at, :] = h
            high, low = split(h)
            w_next[at, pl.ds(0, 128)] = high
            w_next[at, pl.ds(128, 128)] = low
        for base, where in ((0, line_node), (LINES, conv_node), (LINES + CONV, port_node)):
            for k in range(where.shape[1]):
                probe[pl.ds(base + k, 1), :] = volt[pl.ds(where[0, k], 1), :]
        emf = probe[pl.ds(LINES, CONV), :]
        new_axial = axial + rate * (setpoint[0] - axial) - (SAG_FACTOR * cos) * emf
        new_normal = normal + rate * (setpoint[1] - normal) + (SAG_FACTOR * sin) * emf
        state_out[0] = jnp.where(live, limit * jnp.tanh(new_axial * inverse), axial)
        state_out[1] = jnp.where(live, limit * jnp.tanh(new_normal * inverse), normal)
        waves[t] = line_adm * probe[pl.ds(0, LINES), :] - inward
        flow = source - padm * probe[pl.ds(LINES + CONV, PORTS), :]
        current[0] = current[0] + flow * cos
        current[1] = current[1] - flow * sin

    def pair(i, _):
        step(2 * i, w_even, w_odd)
        step(2 * i + 1, w_odd, w_even)
        return 0

    lax.fori_loop(0, STEPS // 2, pair, 0)
    current[...] = current[...] * (2.0 / STEPS)


def window(angle, whole_numbers, ginv, hist0, arrivals, gcap, state, setpoint, pvolt, nodes_of, coefficients):
    nodes, cases = hist0.shape
    smem = pl.BlockSpec(memory_space=pltpu.SMEM)
    vmem = pl.BlockSpec(memory_space=pltpu.VMEM)
    chunks = 8
    scalars = (angle, *whole_numbers, *nodes_of)
    far = (ginv, hist0, gcap, state, setpoint, pvolt)
    rows = (*arrivals, *nodes_of, *coefficients)
    return pl.pallas_call(
        window_kernel,
        out_shape=(
            jax.ShapeDtypeStruct((STEPS, LINES, cases), F32),
            jax.ShapeDtypeStruct((nodes, cases), F32),
            jax.ShapeDtypeStruct(state.shape, F32),
            jax.ShapeDtypeStruct((2, PORTS, cases), F32),
        ),
        in_specs=[smem] * len(scalars)
        + [pl.BlockSpec(memory_space=pltpu.HBM)] * len(far)
        + [vmem] * len(rows),
        out_specs=(vmem,) * 4,
        scratch_shapes=[
            pltpu.VMEM((chunks, nodes // chunks, nodes), F32),
            pltpu.VMEM((nodes, nodes + 256), BF16),
            pltpu.VMEM((nodes, nodes), BF16),
            pltpu.VMEM((LINES, HIST, cases), F32),
            pltpu.VMEM((STEPS, LINES, cases), F32),
            pltpu.VMEM((nodes + 256, 256), BF16),
            pltpu.VMEM((nodes + 256, 256), BF16),
            pltpu.VMEM((nodes, cases), F32),
            pltpu.VMEM((PROBES, cases), F32),
            pltpu.VMEM((128, cases), F32),
            pltpu.VMEM((nodes, cases), F32),
            pltpu.VMEM((2, 128, cases), F32),
            pltpu.VMEM(setpoint.shape, F32),
            pltpu.VMEM(pvolt.shape, F32),
            pltpu.VMEM(gcap.shape, F32),
            pltpu.VMEM((8, 128), jnp.int32),
            pltpu.VMEM((8, 128), F32),
            pltpu.SemaphoreType.DMA((chunks,)),
            pltpu.SemaphoreType.DMA((4,)),
            pltpu.SemaphoreType.DMA((5,)),
        ],
        compiler_params=pltpu.CompilerParams(vmem_limit_bytes=59 << 20),
        cost_estimate=pl.CostEstimate(
            flops=6 * STEPS * nodes * nodes * cases,
            bytes_accessed=64 << 20,
            transcendentals=0,
        ),
        name="window",
    )(*scalars, *far, *rows)


def spread_kernel(current, impedance, out):
    for i in range(out.shape[0]):
        out[i] = current[...]


def spread(current, impedance, size):
    vmem = pl.BlockSpec(memory_space=pltpu.VMEM)
    return pl.pallas_call(
        spread_kernel,
        out_shape=jax.ShapeDtypeStruct((size, *current.shape), F32),
        in_specs=[vmem, pl.BlockSpec(memory_space=pl.ANY)],
        out_specs=vmem,
        compiler_params=pltpu.CompilerParams(vmem_limit_bytes=16 << 20),
        name="spread_currents",
    )(current, impedance)


def bus_kernel(impedance, current, out):
    members, areas = current.shape[:2]
    rows = pl.ds(0, out.shape[0] * out.shape[2])
    z = jnp.concatenate([impedance[i, rows, :] for i in range(areas)], axis=1)
    parts = []
    for i in range(areas):
        real = jnp.concatenate([current[r, i, 0] for r in range(members)], axis=0)
        imag = jnp.concatenate([current[r, i, 1] for r in range(members)], axis=0)
        parts.append(jnp.concatenate([real, imag], axis=1))
        parts.append(jnp.concatenate([-imag, real], axis=1))
    w = jnp.concatenate(parts, axis=0)
    z_high, z_low = split(z)
    w_high, w_low = split(w)
    volts = dot(z_high, w_high) + dot(z_low, w_high) + dot(z_high, w_low)
    size = out.shape[2]
    for i in range(out.shape[0]):
        for k in range(2):
            out[i, k] = volts[i * size : (i + 1) * size, k * 128 : (k + 1) * 128]


def bus_product(impedance, current, pieces):
    vmem = pl.BlockSpec(memory_space=pltpu.VMEM)
    return pl.pallas_call(
        bus_kernel,
        out_shape=jax.ShapeDtypeStruct(
            (pieces, 2, (impedance.shape[1] - 8) // pieces, 128), F32
        ),
        in_specs=[vmem] * 2,
        out_specs=vmem,
        compiler_params=pltpu.CompilerParams(vmem_limit_bytes=32 << 20),
        name="bus_product",
    )(impedance, current)


def port_kernel(first, ports, volts, out):
    rows = volts.shape[1]
    both = jnp.concatenate([volts[0], volts[1]], axis=1)
    high, rest = split(both)
    middle = both - high.astype(F32)
    low = (middle - rest.astype(F32)).astype(BF16)
    row = lax.broadcasted_iota(jnp.int32, (rows, 128), 0) + first[0]
    for area in range(ports.shape[0]):
        wanted = ports[area, pl.ds(rows, 1), :].astype(jnp.int32)
        picks = jnp.where(row == wanted, 1.0, 0.0).T.astype(BF16)
        found = dot(picks, high) + dot(picks, rest) + dot(picks, low)
        for member in range(out.shape[0]):
            out[member, area] = found[member * PORTS : (member + 1) * PORTS]


def port_rows(first, ports, volts, members):
    vmem = pl.BlockSpec(memory_space=pltpu.VMEM)
    return pl.pallas_call(
        port_kernel,
        out_shape=jax.ShapeDtypeStruct((members, ports.shape[0], PORTS, 2 * volts.shape[2]), F32),
        in_specs=[pl.BlockSpec(memory_space=pltpu.SMEM), vmem, vmem],
        out_specs=vmem,
        compiler_params=pltpu.CompilerParams(vmem_limit_bytes=32 << 20),
        name="port_rows",
    )(first, ports, volts)


def shifted(x, by):
    size = lax.axis_size(ALL)
    return lax.ppermute(x, ALL, [(i, (i + by) % size) for i in range(size)])


def copy_for_each(x, axis):
    size = lax.axis_size(axis)
    return lax.all_to_all(jnp.broadcast_to(x[None], (size, *x.shape)), axis, 0, 0, tiled=True)


def per_device(
    conductance_inverse,
    cap_history,
    cap_conductance,
    wave_history,
    line_partner,
    line_node,
    line_delay,
    line_admittance,
    conv_node,
    conv_count,
    conv_state,
    conv_reference,
    conv_rate,
    conv_limit,
    port_node,
    port_admittance,
    port_voltage_prev,
    port_bus,
    transfer_impedance,
):
    areas = lax.axis_size("z")
    members = lax.axis_size(ROW)
    bus_rows = transfer_impedance.shape[1]
    with jax.named_scope("wave_exchange"):
        near_up, far_up, near_down, far_down = pack(line_partner, wave_history[0])
        arrivals = (
            shifted(near_up, 1),
            shifted(far_up, 2),
            shifted(near_down, -1),
            shifted(far_down, -2),
        )
    with jax.named_scope("impedance_exchange"):
        ports = port_bus.reshape(1, -1).astype(F32)
        ports = jnp.pad(ports, ((0, 0), (0, 128 - ports.shape[1])), constant_values=-1.0)
        blocks = turn(jnp.swapaxes(transfer_impedance, 1, 2), ports, arrivals, areas)
        impedance = lax.all_to_all(blocks, "z", 0, 0, tiled=True)
    with jax.named_scope("window"):
        theta = np.arange(1, STEPS + 1, dtype=np.float32) * np.float32(2.0 * math.pi / STEPS)
        angle = jnp.asarray(np.stack([np.cos(theta), np.sin(theta)]).astype(np.float32))
        outward, hist_end, conv_out, current = window(
            angle,
            (line_partner, line_delay, conv_count),
            conductance_inverse[0],
            cap_history[0],
            arrivals,
            cap_conductance,
            conv_state[0],
            conv_reference[0],
            port_voltage_prev[:, 0],
            (line_node, conv_node, port_node),
            (line_admittance, conv_limit, conv_rate, port_admittance),
        )
    with jax.named_scope("currents"):
        flat = spread(current, impedance, areas)
        flat = copy_for_each(lax.all_to_all(flat, "z", 0, 0, tiled=True), ROW)
        flat = flat.reshape(members, areas, *current.shape)
    with jax.named_scope("bus_voltage"):
        pieces = bus_product(impedance, flat, lax.axis_size("x"))
        own = jnp.sum(lax.all_to_all(pieces, "x", 0, 0, tiled=True), axis=0)
        block = jnp.moveaxis(copy_for_each(own, "x"), 0, 1)
        block = block.reshape(2, -1, block.shape[-1])
        bus_voltage = lax.all_gather(block, "z", axis=1, tiled=True)
    with jax.named_scope("port_voltage"):
        first = lax.axis_index(ROW) * bus_rows + lax.axis_index("z") * block.shape[1]
        picked = port_rows(first[None].astype(jnp.int32), impedance, block, members)
        mine = jnp.sum(lax.all_to_all(picked, ROW, 0, 0, tiled=True), axis=0)
        mine = jnp.sum(lax.all_to_all(mine, "z", 0, 0, tiled=True), axis=0)
        cases = mine.shape[1] // 2
        port_voltage = jnp.stack([mine[:, :cases], mine[:, cases:]])[:, None]
    return (outward[None], hist_end[None], conv_out[None], bus_voltage, port_voltage)


def solution(mesh):
    devices = mesh.devices.reshape(8, 4, 4, 2)
    torus = Mesh(devices, ALL)
    return jax.shard_map(
        per_device,
        mesh=torus,
        in_specs=(
            P(ALL, None, None),
            P(ALL, None, None),
            P(ALL, None),
            P(ALL, None, None, None),
            P(ALL, None),
            P(ALL, None),
            P(ALL, None),
            P(ALL, None),
            P(ALL, None),
            P(ALL),
            P(ALL, None, None, None),
            P(ALL, None, None, None),
            P(ALL, None),
            P(ALL, None),
            P(ALL, None),
            P(ALL, None),
            P(None, ALL, None, None),
            P(AREA, None),
            P(None, ROW, AREA),
        ),
        out_specs=(
            P(ALL, None, None, None),
            P(ALL, None, None),
            P(ALL, None, None, None),
            P(None, ROW, None),
            P(None, ALL, None, None),
        ),
        check_vma=False,
    )
```

```python
import math

import jax
import jax.numpy as jnp
import numpy as np
from jax import lax
from jax.experimental import pallas as pl
from jax.experimental.pallas import tpu as pltpu
from jax.sharding import Mesh
from jax.sharding import PartitionSpec as P

STEPS = 20
HIST = 40
NEAR = 12
LINES = 32
CONV = 64
PORTS = 8
HALF = LINES // 2
PROBES = LINES + CONV + PORTS
SAG_FACTOR = 0.3
UNROLL = 4
ALL = ("z", "x", "y", "core")
AREA = ("z", "x")
ROW = ("y", "core")
F32 = jnp.float32
BF16 = jnp.bfloat16


def dot(a, b):
    return jnp.dot(a, b, preferred_element_type=F32)


def split(x):
    high = x.astype(BF16)
    return high, (x - high.astype(F32)).astype(BF16)


def reach_of(partner, line):
    return jnp.bitwise_and(partner[0, line] - partner[0, HALF + line], 255) // 2


def pack_kernel(partner, waves, near_up, far_up, near_down, far_down):
    near = jnp.int32(0)
    for line in range(HALF):
        is_near = reach_of(partner, line) == 1
        up = waves[:, line, :]
        down = waves[:, line + HALF, :]

        @pl.when(is_near)
        def _(near=near, up=up, down=down):
            near_up[near] = up
            near_down[near] = down

        @pl.when(jnp.logical_not(is_near))
        def _(far=line - near, up=up, down=down):
            far_up[far] = up
            far_down[far] = down

        near = near + is_near.astype(jnp.int32)


def pack(partner, waves):
    hist, _, cases = waves.shape
    near = jax.ShapeDtypeStruct((NEAR, hist, cases), F32)
    far = jax.ShapeDtypeStruct((HALF - NEAR, hist, cases), F32)
    vmem = pl.BlockSpec(memory_space=pltpu.VMEM)
    return pl.pallas_call(
        pack_kernel,
        out_shape=(near, far, near, far),
        in_specs=[pl.BlockSpec(memory_space=pltpu.SMEM), vmem],
        out_specs=(vmem,) * 4,
        compiler_params=pltpu.CompilerParams(vmem_limit_bytes=32 << 20),
        name="pack_waves",
    )(partner, waves)


def turn_kernel(impedance, ports, *rest):
    blocks = rest[-1]
    areas, rows, _ = blocks.shape
    rows = rows - 8
    for first in range(0, areas * rows, 128):
        part = impedance[:, :, pl.ds(first, 128)]
        turned = jnp.concatenate([part[0], part[1]], axis=0).T
        done = 0
        while done < 128:
            area, at = divmod(first + done, rows)
            size = min(128 - done, rows - at)
            blocks[area, pl.ds(at, size), :] = turned[done : done + size]
            done += size
    for area in range(areas):
        blocks[area, pl.ds(rows, 8), :] = jnp.broadcast_to(ports[...], (8, 128))


def turn(impedance, ports, arrivals, areas):
    vmem = pl.BlockSpec(memory_space=pltpu.VMEM)
    return pl.pallas_call(
        turn_kernel,
        out_shape=jax.ShapeDtypeStruct((areas, impedance.shape[2] // areas + 8, 128), F32),
        in_specs=[vmem] * (2 + len(arrivals)),
        out_specs=vmem,
        compiler_params=pltpu.CompilerParams(vmem_limit_bytes=32 << 20),
        name="turn_impedance",
    )(impedance, ports, *arrivals)


def column(row):
    return jnp.broadcast_to(row, (128, 128)).T


def window_kernel(
    angle,
    partner,
    delay,
    count,
    line_node,
    conv_node,
    port_node,
    g_hbm,
    hist0_hbm,
    gcap_hbm,
    state0_hbm,
    setpoint_hbm,
    pvolt_hbm,
    near_up,
    far_up,
    near_down,
    far_down,
    line_nodes,
    conv_nodes,
    port_nodes,
    line_adms,
    limits,
    rates,
    port_adms,
    waves,
    hist_out,
    state_out,
    current,
    g_in,
    g_high,
    g_low,
    arrived,
    incoming,
    w_even,
    w_odd,
    volt,
    probe,
    stack,
    cap2,
    coef,
    setpoint,
    pvolt,
    gcap,
    nodes_row,
    coef_row,
    g_sem,
    a_sem,
    s_sem,
):
    nodes = g_high.shape[0]
    chunks = g_in.shape[0]
    rows = nodes // chunks
    small = []

    def bring(source, target):
        small.append(pltpu.make_async_copy(source, target, s_sem.at[len(small)]))
        small[-1].start()

    bring(gcap_hbm, gcap)
    bring(hist0_hbm, hist_out)
    bring(state0_hbm, state_out)
    bring(setpoint_hbm, setpoint)
    bring(pvolt_hbm, pvolt)
    copies = [
        pltpu.make_async_copy(g_hbm.at[pl.ds(i * rows, rows)], g_in.at[i], g_sem.at[i])
        for i in range(chunks)
    ]
    for copy in copies:
        copy.start()
    first = 0
    moves = []
    for i, part in enumerate((near_up, far_up, near_down, far_down)):
        size = part.shape[0]
        moves.append(
            pltpu.make_async_copy(part, arrived.at[pl.ds(first, size)], a_sem.at[i])
        )
        first += size
    for move in moves:
        move.start()

    zeros = jnp.zeros((256, 128), BF16)
    for w in (w_even, w_odd):
        w[pl.ds(nodes, 256), pl.ds(0, 128)] = zeros
        w[pl.ds(nodes, 256), pl.ds(128, 128)] = zeros
    current[...] = jnp.zeros_like(current)
    stack[...] = jnp.zeros_like(stack)
    nodes_row[...] = jnp.full(nodes_row.shape, -1, jnp.int32)
    coef_row[...] = jnp.ones(coef_row.shape, F32)
    for copy in small:
        copy.wait()

    at_conv, at_port = pl.ds(LINES, CONV), pl.ds(LINES + CONV, PORTS)
    first_row = pl.ds(0, 1)
    nodes_row[first_row, pl.ds(0, LINES)] = line_nodes[...]
    nodes_row[first_row, at_conv] = conv_nodes[...]
    nodes_row[first_row, at_port] = port_nodes[...]
    coef_row[first_row, pl.ds(0, LINES)] = line_adms[...]
    coef_row[first_row, at_conv] = limits[...]
    coef_row[first_row, at_port] = port_adms[...]
    coef_row[pl.ds(1, 1), at_conv] = rates[...]
    coef[0] = column(coef_row[pl.ds(0, 1), :])
    coef[1] = column(coef_row[pl.ds(1, 1), :])
    for i in range(nodes // 128):
        cap2[pl.ds(i * 128, 128)] = 2.0 * column(gcap[:, pl.ds(i * 128, 128)])
    high, low = split(hist_out[...])
    w_even[pl.ds(0, nodes), pl.ds(0, 128)] = high
    w_even[pl.ds(0, nodes), pl.ds(128, 128)] = low

    picks = (
        lax.broadcasted_iota(jnp.int32, (nodes, 128), 0) == nodes_row[pl.ds(0, 1), :]
    ).astype(BF16)
    for i, copy in enumerate(copies):
        copy.wait()
        high, low = split(g_in[i])
        at = pl.ds(i * rows, rows)
        g_high[at, pl.ds(0, nodes)] = high
        g_low[at, :] = low

    half = nodes // 2
    for i in range(0, nodes, half):
        at = pl.ds(i, half)
        g_high[at, pl.ds(nodes, 128)] = dot(g_high[at, pl.ds(0, nodes)], picks).astype(BF16)
        g_high[at, pl.ds(nodes + 128, 128)] = dot(g_low[at, :], picks).astype(BF16)

    for move in moves:
        move.wait()
    near = jnp.int32(0)
    for line in range(HALF):
        is_near = reach_of(partner, line) == 1
        place = jnp.where(is_near, near, NEAR + line - near)
        near = near + is_near.astype(jnp.int32)
        for slot, at in ((line + HALF, place), (line, place + HALF)):
            start = HIST - delay[0, slot]
            incoming[:, slot, :] = arrived[at, pl.ds(start, STEPS), :]

    line_adm = 2.0 * coef[0, :LINES]
    limit = coef[0, LINES : LINES + CONV]
    padm = coef[0, LINES + CONV : PROBES]
    rate = coef[1, LINES : LINES + CONV]
    inverse = 1.0 / limit
    live = lax.broadcasted_iota(jnp.int32, (CONV, 128), 0) < count[0]

    def step(t, w, w_next):
        cos, sin = angle[0, t], angle[1, t]
        axial, normal = state_out[0], state_out[1]
        inward = incoming[t]
        source = padm * (pvolt[0] * cos - pvolt[1] * sin)
        stack[pl.ds(0, LINES)] = inward
        stack[pl.ds(LINES, CONV)] = jnp.where(live, axial * cos - normal * sin, 0.0)
        stack[pl.ds(LINES + CONV, PORTS)] = source
        high, low = split(stack[...])
        w[pl.ds(nodes, 128), pl.ds(0, 128)] = high
        w[pl.ds(nodes, 128), pl.ds(128, 128)] = low
        w[pl.ds(nodes + 128, 128), pl.ds(0, 128)] = high
        block = 256
        for i in range(0, nodes, block):
            at = pl.ds(i, block)
            y = dot(g_high[at, :], w[...])
            z = dot(g_low[at, :], w[pl.ds(0, nodes), pl.ds(0, 128)])
            v = y[:, :128] + y[:, 128:] + z
            volt[at, :] = v
            h = cap2[at, :] * v - hist_out[at, :]
            hist_out[at, :] = h
            high, low = split(h)
            w_next[at, pl.ds(0, 128)] = high
            w_next[at, pl.ds(128, 128)] = low
        for base, where in ((0, line_node), (LINES, conv_node), (LINES + CONV, port_node)):
            for k in range(where.shape[1]):
                probe[pl.ds(base + k, 1), :] = volt[pl.ds(where[0, k], 1), :]
        emf = probe[pl.ds(LINES, CONV), :]
        new_axial = axial + rate * (setpoint[0] - axial) - (SAG_FACTOR * cos) * emf
        new_normal = normal + rate * (setpoint[1] - normal) + (SAG_FACTOR * sin) * emf
        state_out[0] = jnp.where(live, limit * jnp.tanh(new_axial * inverse), axial)
        state_out[1] = jnp.where(live, limit * jnp.tanh(new_normal * inverse), normal)
        waves[t] = line_adm * probe[pl.ds(0, LINES), :] - inward
        flow = source - padm * probe[pl.ds(LINES + CONV, PORTS), :]
        current[0] = current[0] + flow * cos
        current[1] = current[1] - flow * sin

    def several(i, _):
        for j in range(0, UNROLL, 2):
            step(UNROLL * i + j, w_even, w_odd)
            step(UNROLL * i + j + 1, w_odd, w_even)
        return 0

    lax.fori_loop(0, STEPS // UNROLL, several, 0)
    current[...] = current[...] * (2.0 / STEPS)


def window(angle, whole_numbers, ginv, hist0, arrivals, gcap, state, setpoint, pvolt, nodes_of, coefficients):
    nodes, cases = hist0.shape
    smem = pl.BlockSpec(memory_space=pltpu.SMEM)
    vmem = pl.BlockSpec(memory_space=pltpu.VMEM)
    chunks = 8
    scalars = (angle, *whole_numbers, *nodes_of)
    far = (ginv, hist0, gcap, state, setpoint, pvolt)
    rows = (*arrivals, *nodes_of, *coefficients)
    return pl.pallas_call(
        window_kernel,
        out_shape=(
            jax.ShapeDtypeStruct((STEPS, LINES, cases), F32),
            jax.ShapeDtypeStruct((nodes, cases), F32),
            jax.ShapeDtypeStruct(state.shape, F32),
            jax.ShapeDtypeStruct((2, PORTS, cases), F32),
        ),
        in_specs=[smem] * len(scalars)
        + [pl.BlockSpec(memory_space=pltpu.HBM)] * len(far)
        + [vmem] * len(rows),
        out_specs=(vmem,) * 4,
        scratch_shapes=[
            pltpu.VMEM((chunks, nodes // chunks, nodes), F32),
            pltpu.VMEM((nodes, nodes + 256), BF16),
            pltpu.VMEM((nodes, nodes), BF16),
            pltpu.VMEM((LINES, HIST, cases), F32),
            pltpu.VMEM((STEPS, LINES, cases), F32),
            pltpu.VMEM((nodes + 256, 256), BF16),
            pltpu.VMEM((nodes + 256, 256), BF16),
            pltpu.VMEM((nodes, cases), F32),
            pltpu.VMEM((PROBES, cases), F32),
            pltpu.VMEM((128, cases), F32),
            pltpu.VMEM((nodes, cases), F32),
            pltpu.VMEM((2, 128, cases), F32),
            pltpu.VMEM(setpoint.shape, F32),
            pltpu.VMEM(pvolt.shape, F32),
            pltpu.VMEM(gcap.shape, F32),
            pltpu.VMEM((8, 128), jnp.int32),
            pltpu.VMEM((8, 128), F32),
            pltpu.SemaphoreType.DMA((chunks,)),
            pltpu.SemaphoreType.DMA((4,)),
            pltpu.SemaphoreType.DMA((5,)),
        ],
        compiler_params=pltpu.CompilerParams(vmem_limit_bytes=59 << 20),
        cost_estimate=pl.CostEstimate(
            flops=6 * STEPS * nodes * nodes * cases,
            bytes_accessed=64 << 20,
            transcendentals=0,
        ),
        name="window",
    )(*scalars, *far, *rows)


def spread_kernel(current, impedance, out):
    for i in range(out.shape[0]):
        out[i] = current[...]


def spread(current, impedance, size):
    vmem = pl.BlockSpec(memory_space=pltpu.VMEM)
    return pl.pallas_call(
        spread_kernel,
        out_shape=jax.ShapeDtypeStruct((size, *current.shape), F32),
        in_specs=[vmem, pl.BlockSpec(memory_space=pl.ANY)],
        out_specs=vmem,
        compiler_params=pltpu.CompilerParams(vmem_limit_bytes=16 << 20),
        name="spread_currents",
    )(current, impedance)


def bus_kernel(place, impedance, own, other, out, gathered):
    chips, areas = own.shape[:2]
    y, core = place[0], place[1]
    for k in range(chips):
        row = lax.rem(y - k + chips, chips) * 2
        for i in range(areas):
            for part in range(2):
                gathered[i, part, row + core] = own[k, i, part]
                gathered[i, part, row + 1 - core] = other[k, i, part]
    rows = pl.ds(0, out.shape[1])
    z = jnp.concatenate([impedance[i, rows, :] for i in range(areas)], axis=1)
    parts = []
    for i in range(areas):
        real = gathered[i, 0].reshape(-1, 128)
        imag = gathered[i, 1].reshape(-1, 128)
        parts.append(jnp.concatenate([real, imag], axis=1))
        parts.append(jnp.concatenate([-imag, real], axis=1))
    w = jnp.concatenate(parts, axis=0)
    z_high, z_low = split(z)
    w_high, w_low = split(w)
    volts = dot(z_high, w_high) + dot(z_low, w_high) + dot(z_high, w_low)
    out[0] = volts[:, :128]
    out[1] = volts[:, 128:]


def bus_product(place, impedance, own, other):
    chips, areas, _, ports, cases = own.shape
    vmem = pl.BlockSpec(memory_space=pltpu.VMEM)
    return pl.pallas_call(
        bus_kernel,
        out_shape=jax.ShapeDtypeStruct((2, impedance.shape[1] - 8, cases), F32),
        in_specs=[pl.BlockSpec(memory_space=pltpu.SMEM)] + [vmem] * 3,
        out_specs=vmem,
        scratch_shapes=[pltpu.VMEM((areas, 2, 2 * chips, ports, cases), F32)],
        compiler_params=pltpu.CompilerParams(vmem_limit_bytes=32 << 20),
        name="bus_product",
    )(place, impedance, own, other)


def sum_kernel(*refs):
    total = refs[0][...]
    for ref in refs[1:-1]:
        total = total + ref[...]
    refs[-1][...] = total


def sum_of(parts):
    vmem = pl.BlockSpec(memory_space=pltpu.VMEM)
    return pl.pallas_call(
        sum_kernel,
        out_shape=jax.ShapeDtypeStruct(parts[0].shape, F32),
        in_specs=[vmem] * len(parts),
        out_specs=vmem,
        compiler_params=pltpu.CompilerParams(vmem_limit_bytes=16 << 20),
        name="sum_of_parts",
    )(*parts)


def port_kernel(first, ports, volts, out):
    rows = volts.shape[1]
    both = jnp.concatenate([volts[0], volts[1]], axis=1)
    high, rest = split(both)
    middle = both - high.astype(F32)
    low = (middle - rest.astype(F32)).astype(BF16)
    row = lax.broadcasted_iota(jnp.int32, (rows, 128), 0) + first[0]
    for area in range(ports.shape[0]):
        wanted = ports[area, pl.ds(rows, 1), :].astype(jnp.int32)
        picks = jnp.where(row == wanted, 1.0, 0.0).T.astype(BF16)
        found = dot(picks, high) + dot(picks, rest) + dot(picks, low)
        for member in range(out.shape[0]):
            out[member, area] = found[member * PORTS : (member + 1) * PORTS]


def port_rows(first, ports, volts, members):
    vmem = pl.BlockSpec(memory_space=pltpu.VMEM)
    return pl.pallas_call(
        port_kernel,
        out_shape=jax.ShapeDtypeStruct((members, ports.shape[0], PORTS, 2 * volts.shape[2]), F32),
        in_specs=[pl.BlockSpec(memory_space=pltpu.SMEM), vmem, vmem],
        out_specs=vmem,
        compiler_params=pltpu.CompilerParams(vmem_limit_bytes=32 << 20),
        name="port_rows",
    )(first, ports, volts)


def shifted(x, by):
    size = lax.axis_size(ALL)
    return lax.ppermute(x, ALL, [(i, (i + by) % size) for i in range(size)])


def along(x, axis, by):
    size = lax.axis_size(axis)
    return lax.ppermute(x, axis, [(i, (i + by) % size) for i in range(size)])


def from_all(x, axis):
    near, far, back = (along(x, axis, by) for by in (1, 3, 2))
    return x, near, back, far


def per_device(
    conductance_inverse,
    cap_history,
    cap_conductance,
    wave_history,
    line_partner,
    line_node,
    line_delay,
    line_admittance,
    conv_node,
    conv_count,
    conv_state,
    conv_reference,
    conv_rate,
    conv_limit,
    port_node,
    port_admittance,
    port_voltage_prev,
    port_bus,
    transfer_impedance,
):
    areas = lax.axis_size("z")
    members = lax.axis_size(ROW)
    bus_rows = transfer_impedance.shape[1]
    with jax.named_scope("wave_exchange"):
        near_up, far_up, near_down, far_down = pack(line_partner, wave_history[0])
        arrivals = (
            shifted(near_up, 1),
            shifted(far_up, 2),
            shifted(near_down, -1),
            shifted(far_down, -2),
        )
    with jax.named_scope("impedance_exchange"):
        ports = port_bus.reshape(1, -1).astype(F32)
        ports = jnp.pad(ports, ((0, 0), (0, 128 - ports.shape[1])), constant_values=-1.0)
        blocks = turn(jnp.swapaxes(transfer_impedance, 1, 2), ports, arrivals, areas)
        impedance = lax.all_to_all(blocks, "z", 0, 0, tiled=True)
    with jax.named_scope("window"):
        theta = np.arange(1, STEPS + 1, dtype=np.float32) * np.float32(2.0 * math.pi / STEPS)
        angle = jnp.asarray(np.stack([np.cos(theta), np.sin(theta)]).astype(np.float32))
        outward, hist_end, conv_out, current = window(
            angle,
            (line_partner, line_delay, conv_count),
            conductance_inverse[0],
            cap_history[0],
            arrivals,
            cap_conductance,
            conv_state[0],
            conv_reference[0],
            port_voltage_prev[:, 0],
            (line_node, conv_node, port_node),
            (line_admittance, conv_limit, conv_rate, port_admittance),
        )
    with jax.named_scope("currents"):
        flat = spread(current, impedance, areas)
        flat = lax.all_to_all(flat, "z", 0, 0, tiled=True)
        own = jnp.stack(from_all(flat, "y"))
        other = along(own, "core", 1)
        place = jnp.stack([lax.axis_index("y"), lax.axis_index("core")]).astype(jnp.int32)
    with jax.named_scope("bus_voltage"):
        partial = bus_product(place, impedance, own, other)
        block = sum_of(from_all(partial, "x"))
        bus_voltage = lax.all_gather(block, "z", axis=1, tiled=True)
    with jax.named_scope("port_voltage"):
        first = lax.axis_index(ROW) * bus_rows + lax.axis_index("z") * block.shape[1]
        picked = port_rows(first[None].astype(jnp.int32), impedance, block, members)
        mine = jnp.sum(lax.all_to_all(picked, ROW, 0, 0, tiled=True), axis=0)
        mine = jnp.sum(lax.all_to_all(mine, "z", 0, 0, tiled=True), axis=0)
        cases = mine.shape[1] // 2
        port_voltage = jnp.stack([mine[:, :cases], mine[:, cases:]])[:, None]
    return (outward[None], hist_end[None], conv_out[None], bus_voltage, port_voltage)


def solution(mesh):
    devices = mesh.devices.reshape(8, 4, 4, 2)
    torus = Mesh(devices, ALL)
    return jax.shard_map(
        per_device,
        mesh=torus,
        in_specs=(
            P(ALL, None, None),
            P(ALL, None, None),
            P(ALL, None),
            P(ALL, None, None, None),
            P(ALL, None),
            P(ALL, None),
            P(ALL, None),
            P(ALL, None),
            P(ALL, None),
            P(ALL),
            P(ALL, None, None, None),
            P(ALL, None, None, None),
            P(ALL, None),
            P(ALL, None),
            P(ALL, None),
            P(ALL, None),
            P(None, ALL, None, None),
            P(AREA, None),
            P(None, ROW, AREA),
        ),
        out_specs=(
            P(ALL, None, None, None),
            P(ALL, None, None),
            P(ALL, None, None, None),
            P(None, ROW, None),
            P(None, ALL, None, None),
        ),
        check_vma=False,
    )
```

```python
import math

import jax
import jax.numpy as jnp
import numpy as np
from jax import lax
from jax.experimental import pallas as pl
from jax.experimental.pallas import tpu as pltpu
from jax.sharding import Mesh
from jax.sharding import PartitionSpec as P

STEPS = 20
HIST = 40
NEAR = 12
LINES = 32
CONV = 64
PORTS = 8
HALF = LINES // 2
PROBES = LINES + CONV + PORTS
SAG_FACTOR = 0.3
UNROLL = 4
ALL = ("z", "x", "y", "core")
AREA = ("z", "x")
ROW = ("y", "core")
F32 = jnp.float32
BF16 = jnp.bfloat16


def dot(a, b):
    return jnp.dot(a, b, preferred_element_type=F32)


def split(x):
    high = x.astype(BF16)
    return high, (x - high.astype(F32)).astype(BF16)


def reach_of(partner, line):
    return jnp.bitwise_and(partner[0, line] - partner[0, HALF + line], 255) // 2


def pack_kernel(partner, waves, near_up, far_down, near_down, far_up):
    near = jnp.int32(0)
    for line in range(HALF):
        is_near = reach_of(partner, line) == 1
        up = waves[:, line, :]
        down = waves[:, line + HALF, :]

        @pl.when(is_near)
        def _(near=near, up=up, down=down):
            near_up[near] = up
            near_down[near] = down

        @pl.when(jnp.logical_not(is_near))
        def _(far=line - near, up=up, down=down):
            far_up[far] = up
            far_down[far] = down

        near = near + is_near.astype(jnp.int32)


def pack(partner, waves):
    hist, _, cases = waves.shape
    near = jax.ShapeDtypeStruct((NEAR, hist, cases), F32)
    far = jax.ShapeDtypeStruct((HALF - NEAR, hist, cases), F32)
    vmem = pl.BlockSpec(memory_space=pltpu.VMEM)
    return pl.pallas_call(
        pack_kernel,
        out_shape=(near, far, near, far),
        in_specs=[pl.BlockSpec(memory_space=pltpu.SMEM), vmem],
        out_specs=(vmem,) * 4,
        compiler_params=pltpu.CompilerParams(vmem_limit_bytes=32 << 20),
        name="pack_waves",
    )(partner, waves)


def turn_kernel(impedance, blocks):
    areas, rows, _ = blocks.shape
    rows = rows - 8
    for first in range(0, areas * rows, 128):
        part = impedance[:, :, pl.ds(first, 128)]
        turned = jnp.concatenate([part[0], part[1]], axis=0).T
        done = 0
        while done < 128:
            area, at = divmod(first + done, rows)
            size = min(128 - done, rows - at)
            blocks[area, pl.ds(at, size), :] = turned[done : done + size]
            done += size
    blocks[:, pl.ds(rows, 8), :] = jnp.zeros((areas, 8, 128), F32)


def turn(impedance, areas):
    vmem = pl.BlockSpec(memory_space=pltpu.VMEM)
    return pl.pallas_call(
        turn_kernel,
        out_shape=jax.ShapeDtypeStruct((areas, impedance.shape[2] // areas + 8, 128), F32),
        in_specs=[vmem],
        out_specs=vmem,
        compiler_params=pltpu.CompilerParams(vmem_limit_bytes=32 << 20),
        name="turn_impedance",
    )(impedance)


def column(row):
    return jnp.broadcast_to(row, (128, 128)).T


def window_kernel(
    angle,
    partner,
    delay,
    count,
    line_node,
    conv_node,
    port_node,
    g_hbm,
    hist0_hbm,
    gcap_hbm,
    state0_hbm,
    setpoint_hbm,
    pvolt_hbm,
    near_up,
    far_down,
    near_down,
    far_up,
    line_nodes,
    conv_nodes,
    port_nodes,
    line_adms,
    limits,
    rates,
    port_adms,
    waves,
    hist_out,
    state_out,
    current,
    g_in,
    g_high,
    g_low,
    arrived,
    incoming,
    w_even,
    w_odd,
    volt,
    probe,
    stack,
    cap2,
    coef,
    setpoint,
    pvolt,
    gcap,
    nodes_row,
    coef_row,
    g_sem,
    a_sem,
    s_sem,
):
    nodes = g_high.shape[0]
    chunks = g_in.shape[0]
    rows = nodes // chunks
    small = []

    def bring(source, target):
        small.append(pltpu.make_async_copy(source, target, s_sem.at[len(small)]))
        small[-1].start()

    bring(gcap_hbm, gcap)
    bring(hist0_hbm, hist_out)
    bring(state0_hbm, state_out)
    bring(setpoint_hbm, setpoint)
    bring(pvolt_hbm, pvolt)
    copies = [
        pltpu.make_async_copy(g_hbm.at[pl.ds(i * rows, rows)], g_in.at[i], g_sem.at[i])
        for i in range(chunks)
    ]
    for copy in copies:
        copy.start()
    first = 0
    moves = []
    for i, part in enumerate((near_up, far_up, near_down, far_down)):
        size = part.shape[0]
        moves.append(
            pltpu.make_async_copy(part, arrived.at[pl.ds(first, size)], a_sem.at[i])
        )
        first += size
    for move in moves:
        move.start()

    zeros = jnp.zeros((256, 128), BF16)
    for w in (w_even, w_odd):
        w[pl.ds(nodes, 256), pl.ds(0, 128)] = zeros
        w[pl.ds(nodes, 256), pl.ds(128, 128)] = zeros
    current[...] = jnp.zeros_like(current)
    stack[...] = jnp.zeros_like(stack)
    nodes_row[...] = jnp.full(nodes_row.shape, -1, jnp.int32)
    coef_row[...] = jnp.ones(coef_row.shape, F32)
    for copy in small:
        copy.wait()

    at_conv, at_port = pl.ds(LINES, CONV), pl.ds(LINES + CONV, PORTS)
    first_row = pl.ds(0, 1)
    nodes_row[first_row, pl.ds(0, LINES)] = line_nodes[...]
    nodes_row[first_row, at_conv] = conv_nodes[...]
    nodes_row[first_row, at_port] = port_nodes[...]
    coef_row[first_row, pl.ds(0, LINES)] = line_adms[...]
    coef_row[first_row, at_conv] = limits[...]
    coef_row[first_row, at_port] = port_adms[...]
    coef_row[pl.ds(1, 1), at_conv] = rates[...]
    coef[0] = column(coef_row[pl.ds(0, 1), :])
    coef[1] = column(coef_row[pl.ds(1, 1), :])
    for i in range(nodes // 128):
        cap2[pl.ds(i * 128, 128)] = 2.0 * column(gcap[:, pl.ds(i * 128, 128)])
    high, low = split(hist_out[...])
    w_even[pl.ds(0, nodes), pl.ds(0, 128)] = high
    w_even[pl.ds(0, nodes), pl.ds(128, 128)] = low

    picks = (
        lax.broadcasted_iota(jnp.int32, (nodes, 128), 0) == nodes_row[pl.ds(0, 1), :]
    ).astype(BF16)
    for i, copy in enumerate(copies):
        copy.wait()
        high, low = split(g_in[i])
        at = pl.ds(i * rows, rows)
        g_high[at, pl.ds(0, nodes)] = high
        g_low[at, :] = low

    half = nodes // 2
    for i in range(0, nodes, half):
        at = pl.ds(i, half)
        g_high[at, pl.ds(nodes, 128)] = dot(g_high[at, pl.ds(0, nodes)], picks).astype(BF16)
        g_high[at, pl.ds(nodes + 128, 128)] = dot(g_low[at, :], picks).astype(BF16)

    for move in moves:
        move.wait()
    near = jnp.int32(0)
    for line in range(HALF):
        is_near = reach_of(partner, line) == 1
        place = jnp.where(is_near, near, NEAR + line - near)
        near = near + is_near.astype(jnp.int32)
        for slot, at in ((line + HALF, place), (line, place + HALF)):
            start = HIST - delay[0, slot]
            incoming[:, slot, :] = arrived[at, pl.ds(start, STEPS), :]

    line_adm = 2.0 * coef[0, :LINES]
    limit = coef[0, LINES : LINES + CONV]
    padm = coef[0, LINES + CONV : PROBES]
    rate = coef[1, LINES : LINES + CONV]
    inverse = 1.0 / limit
    live = lax.broadcasted_iota(jnp.int32, (CONV, 128), 0) < count[0]

    def step(t, w, w_next):
        cos, sin = angle[0, t], angle[1, t]
        axial, normal = state_out[0], state_out[1]
        inward = incoming[t]
        source = padm * (pvolt[0] * cos - pvolt[1] * sin)
        stack[pl.ds(0, LINES)] = inward
        stack[pl.ds(LINES, CONV)] = jnp.where(live, axial * cos - normal * sin, 0.0)
        stack[pl.ds(LINES + CONV, PORTS)] = source
        high, low = split(stack[...])
        w[pl.ds(nodes, 128), pl.ds(0, 128)] = high
        w[pl.ds(nodes, 128), pl.ds(128, 128)] = low
        w[pl.ds(nodes + 128, 128), pl.ds(0, 128)] = high
        block = 256
        for i in range(0, nodes, block):
            at = pl.ds(i, block)
            y = dot(g_high[at, :], w[...])
            z = dot(g_low[at, :], w[pl.ds(0, nodes), pl.ds(0, 128)])
            v = y[:, :128] + y[:, 128:] + z
            volt[at, :] = v
            h = cap2[at, :] * v - hist_out[at, :]
            hist_out[at, :] = h
            high, low = split(h)
            w_next[at, pl.ds(0, 128)] = high
            w_next[at, pl.ds(128, 128)] = low
        for base, where in ((0, line_node), (LINES, conv_node), (LINES + CONV, port_node)):
            for k in range(where.shape[1]):
                probe[pl.ds(base + k, 1), :] = volt[pl.ds(where[0, k], 1), :]
        emf = probe[pl.ds(LINES, CONV), :]
        new_axial = axial + rate * (setpoint[0] - axial) - (SAG_FACTOR * cos) * emf
        new_normal = normal + rate * (setpoint[1] - normal) + (SAG_FACTOR * sin) * emf
        state_out[0] = jnp.where(live, limit * jnp.tanh(new_axial * inverse), axial)
        state_out[1] = jnp.where(live, limit * jnp.tanh(new_normal * inverse), normal)
        waves[t] = line_adm * probe[pl.ds(0, LINES), :] - inward
        flow = source - padm * probe[pl.ds(LINES + CONV, PORTS), :]
        current[0] = current[0] + flow * cos
        current[1] = current[1] - flow * sin

    def several(i, _):
        for j in range(0, UNROLL, 2):
            step(UNROLL * i + j, w_even, w_odd)
            step(UNROLL * i + j + 1, w_odd, w_even)
        return 0

    lax.fori_loop(0, STEPS // UNROLL, several, 0)
    current[...] = current[...] * (2.0 / STEPS)


def window(angle, whole_numbers, ginv, hist0, arrivals, gcap, state, setpoint, pvolt, nodes_of, coefficients):
    nodes, cases = hist0.shape
    smem = pl.BlockSpec(memory_space=pltpu.SMEM)
    vmem = pl.BlockSpec(memory_space=pltpu.VMEM)
    chunks = 8
    scalars = (angle, *whole_numbers, *nodes_of)
    far = (ginv, hist0, gcap, state, setpoint, pvolt)
    rows = (*arrivals, *nodes_of, *coefficients)
    return pl.pallas_call(
        window_kernel,
        out_shape=(
            jax.ShapeDtypeStruct((STEPS, LINES, cases), F32),
            jax.ShapeDtypeStruct((nodes, cases), F32),
            jax.ShapeDtypeStruct(state.shape, F32),
            jax.ShapeDtypeStruct((2, PORTS, cases), F32),
        ),
        in_specs=[smem] * len(scalars)
        + [pl.BlockSpec(memory_space=pltpu.HBM)] * len(far)
        + [vmem] * len(rows),
        out_specs=(vmem,) * 4,
        scratch_shapes=[
            pltpu.VMEM((chunks, nodes // chunks, nodes), F32),
            pltpu.VMEM((nodes, nodes + 256), BF16),
            pltpu.VMEM((nodes, nodes), BF16),
            pltpu.VMEM((LINES, HIST, cases), F32),
            pltpu.VMEM((STEPS, LINES, cases), F32),
            pltpu.VMEM((nodes + 256, 256), BF16),
            pltpu.VMEM((nodes + 256, 256), BF16),
            pltpu.VMEM((nodes, cases), F32),
            pltpu.VMEM((PROBES, cases), F32),
            pltpu.VMEM((128, cases), F32),
            pltpu.VMEM((nodes, cases), F32),
            pltpu.VMEM((2, 128, cases), F32),
            pltpu.VMEM(setpoint.shape, F32),
            pltpu.VMEM(pvolt.shape, F32),
            pltpu.VMEM(gcap.shape, F32),
            pltpu.VMEM((8, 128), jnp.int32),
            pltpu.VMEM((8, 128), F32),
            pltpu.SemaphoreType.DMA((chunks,)),
            pltpu.SemaphoreType.DMA((4,)),
            pltpu.SemaphoreType.DMA((5,)),
        ],
        compiler_params=pltpu.CompilerParams(vmem_limit_bytes=59 << 20),
        cost_estimate=pl.CostEstimate(
            flops=6 * STEPS * nodes * nodes * cases,
            bytes_accessed=64 << 20,
            transcendentals=0,
        ),
        name="window",
    )(*scalars, *far, *rows)


def spread_kernel(current, impedance, out):
    for i in range(out.shape[0]):
        out[i] = current[...]


def spread(current, impedance, size):
    vmem = pl.BlockSpec(memory_space=pltpu.VMEM)
    return pl.pallas_call(
        spread_kernel,
        out_shape=jax.ShapeDtypeStruct((size, *current.shape), F32),
        in_specs=[vmem, pl.BlockSpec(memory_space=pl.ANY)],
        out_specs=vmem,
        compiler_params=pltpu.CompilerParams(vmem_limit_bytes=16 << 20),
        name="spread_currents",
    )(current, impedance)


def bus_kernel(place, impedance, own, other, out, gathered):
    chips, areas = own.shape[:2]
    y, core = place[0], place[1]
    for k in range(chips):
        row = lax.rem(y - k + chips, chips) * 2
        for i in range(areas):
            for part in range(2):
                gathered[i, part, row + core] = own[k, i, part]
                gathered[i, part, row + 1 - core] = other[k, i, part]
    rows = pl.ds(0, out.shape[1])
    z = jnp.concatenate([impedance[i, rows, :] for i in range(areas)], axis=1)
    parts = []
    for i in range(areas):
        real = gathered[i, 0].reshape(-1, 128)
        imag = gathered[i, 1].reshape(-1, 128)
        parts.append(jnp.concatenate([real, imag], axis=1))
        parts.append(jnp.concatenate([-imag, real], axis=1))
    w = jnp.concatenate(parts, axis=0)
    z_high, z_low = split(z)
    w_high, w_low = split(w)
    volts = dot(z_high, w_high) + dot(z_low, w_high) + dot(z_high, w_low)
    out[0] = volts[:, :128]
    out[1] = volts[:, 128:]


def bus_product(place, impedance, own, other):
    chips, areas, _, ports, cases = own.shape
    vmem = pl.BlockSpec(memory_space=pltpu.VMEM)
    return pl.pallas_call(
        bus_kernel,
        out_shape=jax.ShapeDtypeStruct((2, impedance.shape[1] - 8, cases), F32),
        in_specs=[pl.BlockSpec(memory_space=pltpu.SMEM)] + [vmem] * 3,
        out_specs=vmem,
        scratch_shapes=[pltpu.VMEM((areas, 2, 2 * chips, ports, cases), F32)],
        compiler_params=pltpu.CompilerParams(vmem_limit_bytes=32 << 20),
        name="bus_product",
    )(place, impedance, own, other)


def sum_kernel(*refs):
    total = refs[0][...]
    for ref in refs[1:-1]:
        total = total + ref[...]
    refs[-1][...] = total


def sum_of(parts):
    vmem = pl.BlockSpec(memory_space=pltpu.VMEM)
    return pl.pallas_call(
        sum_kernel,
        out_shape=jax.ShapeDtypeStruct(parts[0].shape, F32),
        in_specs=[vmem] * len(parts),
        out_specs=vmem,
        compiler_params=pltpu.CompilerParams(vmem_limit_bytes=16 << 20),
        name="sum_of_parts",
    )(*parts)


def port_kernel(first, ports, volts, out):
    rows = volts.shape[1]
    both = jnp.concatenate([volts[0], volts[1]], axis=1)
    high, rest = split(both)
    middle = both - high.astype(F32)
    low = (middle - rest.astype(F32)).astype(BF16)
    row = lax.broadcasted_iota(jnp.int32, (rows, 128), 0) + first[0]
    for area in range(ports.shape[0]):
        wanted = ports[area, pl.ds(rows, 1), :].astype(jnp.int32)
        picks = jnp.where(row == wanted, 1.0, 0.0).T.astype(BF16)
        found = dot(picks, high) + dot(picks, rest) + dot(picks, low)
        for member in range(out.shape[0]):
            out[member, area] = found[member * PORTS : (member + 1) * PORTS]


def port_rows(first, ports, volts, members):
    vmem = pl.BlockSpec(memory_space=pltpu.VMEM)
    return pl.pallas_call(
        port_kernel,
        out_shape=jax.ShapeDtypeStruct((members, ports.shape[0], PORTS, 2 * volts.shape[2]), F32),
        in_specs=[pl.BlockSpec(memory_space=pltpu.SMEM), vmem, vmem],
        out_specs=vmem,
        compiler_params=pltpu.CompilerParams(vmem_limit_bytes=32 << 20),
        name="port_rows",
    )(first, ports, volts)


def shifted(x, by):
    size = lax.axis_size(ALL)
    return lax.ppermute(x, ALL, [(i, (i + by) % size) for i in range(size)])


def along(x, axis, by):
    size = lax.axis_size(axis)
    return lax.ppermute(x, axis, [(i, (i + by) % size) for i in range(size)])


def from_all(x, axis):
    near, far, back = (along(x, axis, by) for by in (1, 3, 2))
    return x, near, back, far


def per_device(
    conductance_inverse,
    cap_history,
    cap_conductance,
    wave_history,
    line_partner,
    line_node,
    line_delay,
    line_admittance,
    conv_node,
    conv_count,
    conv_state,
    conv_reference,
    conv_rate,
    conv_limit,
    port_node,
    port_admittance,
    port_voltage_prev,
    port_bus,
    transfer_impedance,
):
    areas = lax.axis_size("z")
    members = lax.axis_size(ROW)
    bus_rows = transfer_impedance.shape[1]
    with jax.named_scope("wave_exchange"):
        near_up, far_down, near_down, far_up = pack(line_partner, wave_history[0])
        from_below = shifted(near_up, 1)
        from_above = shifted(near_down, -1)
        from_far_above = shifted(far_down, -2)
        from_far_below = shifted(far_up, 2)
        arrivals = (from_below, from_far_above, from_above, from_far_below)
    with jax.named_scope("impedance_exchange"):
        blocks = turn(jnp.swapaxes(transfer_impedance, 1, 2), areas)
        ports = port_bus.reshape(1, 1, -1).astype(F32)
        ports = jnp.pad(ports, ((0, 0), (0, 0), (0, 128 - ports.shape[2])), constant_values=-1.0)
        ports = ports + 0.0 * sum(x[0, 0, 0] for x in arrivals)
        ports = jnp.broadcast_to(ports, (areas, 8, 128))
        blocks = lax.dynamic_update_slice(blocks, ports, (0, blocks.shape[1] - 8, 0))
        impedance = lax.all_to_all(blocks, "z", 0, 0, tiled=True)
    with jax.named_scope("window"):
        theta = np.arange(1, STEPS + 1, dtype=np.float32) * np.float32(2.0 * math.pi / STEPS)
        angle = jnp.asarray(np.stack([np.cos(theta), np.sin(theta)]).astype(np.float32))
        outward, hist_end, conv_out, current = window(
            angle,
            (line_partner, line_delay, conv_count),
            conductance_inverse[0],
            cap_history[0],
            arrivals,
            cap_conductance,
            conv_state[0],
            conv_reference[0],
            port_voltage_prev[:, 0],
            (line_node, conv_node, port_node),
            (line_admittance, conv_limit, conv_rate, port_admittance),
        )
    with jax.named_scope("currents"):
        flat = spread(current, impedance, areas)
        flat = lax.all_to_all(flat, "z", 0, 0, tiled=True)
        own = jnp.stack(from_all(flat, "y"))
        other = along(own, "core", 1)
        place = jnp.stack([lax.axis_index("y"), lax.axis_index("core")]).astype(jnp.int32)
    with jax.named_scope("bus_voltage"):
        partial = bus_product(place, impedance, own, other)
        block = sum_of(from_all(partial, "x"))
        bus_voltage = lax.all_gather(block, "z", axis=1, tiled=True)
    with jax.named_scope("port_voltage"):
        first = lax.axis_index(ROW) * bus_rows + lax.axis_index("z") * block.shape[1]
        picked = port_rows(first[None].astype(jnp.int32), impedance, block, members)
        mine = jnp.sum(lax.all_to_all(picked, ROW, 0, 0, tiled=True), axis=0)
        mine = jnp.sum(lax.all_to_all(mine, "z", 0, 0, tiled=True), axis=0)
        cases = mine.shape[1] // 2
        port_voltage = jnp.stack([mine[:, :cases], mine[:, cases:]])[:, None]
    return (outward[None], hist_end[None], conv_out[None], bus_voltage, port_voltage)


def solution(mesh):
    devices = mesh.devices.reshape(8, 4, 4, 2)
    torus = Mesh(devices, ALL)
    return jax.shard_map(
        per_device,
        mesh=torus,
        in_specs=(
            P(ALL, None, None),
            P(ALL, None, None),
            P(ALL, None),
            P(ALL, None, None, None),
            P(ALL, None),
            P(ALL, None),
            P(ALL, None),
            P(ALL, None),
            P(ALL, None),
            P(ALL),
            P(ALL, None, None, None),
            P(ALL, None, None, None),
            P(ALL, None),
            P(ALL, None),
            P(ALL, None),
            P(ALL, None),
            P(None, ALL, None, None),
            P(AREA, None),
            P(None, ROW, AREA),
        ),
        out_specs=(
            P(ALL, None, None, None),
            P(ALL, None, None),
            P(ALL, None, None, None),
            P(None, ROW, None),
            P(None, ALL, None, None),
        ),
        check_vma=False,
    )
```

```python
import math

import jax
import jax.numpy as jnp
import numpy as np
from jax import lax
from jax.experimental import pallas as pl
from jax.experimental.pallas import tpu as pltpu
from jax.sharding import Mesh
from jax.sharding import PartitionSpec as P

STEPS = 20
HIST = 40
NEAR = 12
LINES = 32
CONV = 64
PORTS = 8
HALF = LINES // 2
PROBES = LINES + CONV + PORTS
SAG_FACTOR = 0.3
UNROLL = 4
ALL = ("z", "x", "y", "core")
AREA = ("z", "x")
ROW = ("y", "core")
F32 = jnp.float32
BF16 = jnp.bfloat16


def dot(a, b):
    return jnp.dot(a, b, preferred_element_type=F32)


def split(x):
    high = x.astype(BF16)
    return high, (x - high.astype(F32)).astype(BF16)


def reach_of(partner, line):
    return jnp.bitwise_and(partner[0, line] - partner[0, HALF + line], 255) // 2


def pack_kernel(partner, waves, near_up, far_down, near_down, far_up):
    near = jnp.int32(0)
    for line in range(HALF):
        is_near = reach_of(partner, line) == 1
        up = waves[:, line, :]
        down = waves[:, line + HALF, :]

        @pl.when(is_near)
        def _(near=near, up=up, down=down):
            near_up[near] = up
            near_down[near] = down

        @pl.when(jnp.logical_not(is_near))
        def _(far=line - near, up=up, down=down):
            far_up[far] = up
            far_down[far] = down

        near = near + is_near.astype(jnp.int32)


def pack(partner, waves):
    hist, _, cases = waves.shape
    near = jax.ShapeDtypeStruct((NEAR, hist, cases), F32)
    far = jax.ShapeDtypeStruct((HALF - NEAR, hist, cases), F32)
    vmem = pl.BlockSpec(memory_space=pltpu.VMEM)
    return pl.pallas_call(
        pack_kernel,
        out_shape=(near, far, near, far),
        in_specs=[pl.BlockSpec(memory_space=pltpu.SMEM), vmem],
        out_specs=(vmem,) * 4,
        compiler_params=pltpu.CompilerParams(vmem_limit_bytes=32 << 20),
        name="pack_waves",
    )(partner, waves)


def turn_kernel(impedance, blocks):
    areas, rows, _ = blocks.shape
    rows = rows - 8
    for first in range(0, areas * rows, 128):
        part = impedance[:, :, pl.ds(first, 128)]
        turned = jnp.concatenate([part[0], part[1]], axis=0).T
        done = 0
        while done < 128:
            area, at = divmod(first + done, rows)
            size = min(128 - done, rows - at)
            blocks[area, pl.ds(at, size), :] = turned[done : done + size]
            done += size
    blocks[:, pl.ds(rows, 8), :] = jnp.zeros((areas, 8, 128), F32)


def turn(impedance, areas):
    vmem = pl.BlockSpec(memory_space=pltpu.VMEM)
    return pl.pallas_call(
        turn_kernel,
        out_shape=jax.ShapeDtypeStruct((areas, impedance.shape[2] // areas + 8, 128), F32),
        in_specs=[vmem],
        out_specs=vmem,
        compiler_params=pltpu.CompilerParams(vmem_limit_bytes=32 << 20),
        name="turn_impedance",
    )(impedance)


def port_block_kernel(ports, *rest):
    rest[-1][...] = jnp.broadcast_to(ports[...], rest[-1].shape)


def port_block(ports, before, areas):
    vmem = pl.BlockSpec(memory_space=pltpu.VMEM)
    return pl.pallas_call(
        port_block_kernel,
        out_shape=jax.ShapeDtypeStruct((areas, 8, 128), F32),
        in_specs=[vmem] * (1 + len(before)),
        out_specs=vmem,
        compiler_params=pltpu.CompilerParams(vmem_limit_bytes=16 << 20),
        name="port_block",
    )(ports, *before)


def column(row):
    return jnp.broadcast_to(row, (128, 128)).T


def window_kernel(
    angle,
    partner,
    delay,
    count,
    line_node,
    conv_node,
    port_node,
    g_hbm,
    hist0_hbm,
    gcap_hbm,
    state0_hbm,
    setpoint_hbm,
    pvolt_hbm,
    near_up,
    far_down,
    near_down,
    far_up,
    line_nodes,
    conv_nodes,
    port_nodes,
    line_adms,
    limits,
    rates,
    port_adms,
    waves,
    hist_out,
    state_out,
    current,
    g_in,
    g_high,
    g_low,
    arrived,
    incoming,
    w_even,
    w_odd,
    volt,
    probe,
    stack,
    cap2,
    coef,
    setpoint,
    pvolt,
    gcap,
    nodes_row,
    coef_row,
    g_sem,
    a_sem,
    s_sem,
):
    nodes = g_high.shape[0]
    chunks = g_in.shape[0]
    rows = nodes // chunks
    small = []

    def bring(source, target):
        small.append(pltpu.make_async_copy(source, target, s_sem.at[len(small)]))
        small[-1].start()

    bring(gcap_hbm, gcap)
    bring(hist0_hbm, hist_out)
    bring(state0_hbm, state_out)
    bring(setpoint_hbm, setpoint)
    bring(pvolt_hbm, pvolt)
    copies = [
        pltpu.make_async_copy(g_hbm.at[pl.ds(i * rows, rows)], g_in.at[i], g_sem.at[i])
        for i in range(chunks)
    ]
    for copy in copies:
        copy.start()
    first = 0
    moves = []
    for i, part in enumerate((near_up, far_up, near_down, far_down)):
        size = part.shape[0]
        moves.append(
            pltpu.make_async_copy(part, arrived.at[pl.ds(first, size)], a_sem.at[i])
        )
        first += size
    for move in moves:
        move.start()

    zeros = jnp.zeros((256, 128), BF16)
    for w in (w_even, w_odd):
        w[pl.ds(nodes, 256), pl.ds(0, 128)] = zeros
        w[pl.ds(nodes, 256), pl.ds(128, 128)] = zeros
    current[...] = jnp.zeros_like(current)
    stack[...] = jnp.zeros_like(stack)
    nodes_row[...] = jnp.full(nodes_row.shape, -1, jnp.int32)
    coef_row[...] = jnp.ones(coef_row.shape, F32)
    for copy in small:
        copy.wait()

    at_conv, at_port = pl.ds(LINES, CONV), pl.ds(LINES + CONV, PORTS)
    first_row = pl.ds(0, 1)
    nodes_row[first_row, pl.ds(0, LINES)] = line_nodes[...]
    nodes_row[first_row, at_conv] = conv_nodes[...]
    nodes_row[first_row, at_port] = port_nodes[...]
    coef_row[first_row, pl.ds(0, LINES)] = line_adms[...]
    coef_row[first_row, at_conv] = limits[...]
    coef_row[first_row, at_port] = port_adms[...]
    coef_row[pl.ds(1, 1), at_conv] = rates[...]
    coef[0] = column(coef_row[pl.ds(0, 1), :])
    coef[1] = column(coef_row[pl.ds(1, 1), :])
    for i in range(nodes // 128):
        cap2[pl.ds(i * 128, 128)] = 2.0 * column(gcap[:, pl.ds(i * 128, 128)])
    high, low = split(hist_out[...])
    w_even[pl.ds(0, nodes), pl.ds(0, 128)] = high
    w_even[pl.ds(0, nodes), pl.ds(128, 128)] = low

    picks = (
        lax.broadcasted_iota(jnp.int32, (nodes, 128), 0) == nodes_row[pl.ds(0, 1), :]
    ).astype(BF16)
    for i, copy in enumerate(copies):
        copy.wait()
        high, low = split(g_in[i])
        at = pl.ds(i * rows, rows)
        g_high[at, pl.ds(0, nodes)] = high
        g_low[at, :] = low

    half = nodes // 2
    for i in range(0, nodes, half):
        at = pl.ds(i, half)
        g_high[at, pl.ds(nodes, 128)] = dot(g_high[at, pl.ds(0, nodes)], picks).astype(BF16)
        g_high[at, pl.ds(nodes + 128, 128)] = dot(g_low[at, :], picks).astype(BF16)

    for move in moves:
        move.wait()
    near = jnp.int32(0)
    for line in range(HALF):
        is_near = reach_of(partner, line) == 1
        place = jnp.where(is_near, near, NEAR + line - near)
        near = near + is_near.astype(jnp.int32)
        for slot, at in ((line + HALF, place), (line, place + HALF)):
            start = HIST - delay[0, slot]
            incoming[:, slot, :] = arrived[at, pl.ds(start, STEPS), :]

    line_adm = 2.0 * coef[0, :LINES]
    limit = coef[0, LINES : LINES + CONV]
    padm = coef[0, LINES + CONV : PROBES]
    rate = coef[1, LINES : LINES + CONV]
    inverse = 1.0 / limit
    live = lax.broadcasted_iota(jnp.int32, (CONV, 128), 0) < count[0]

    def step(t, w, w_next):
        cos, sin = angle[0, t], angle[1, t]
        axial, normal = state_out[0], state_out[1]
        inward = incoming[t]
        source = padm * (pvolt[0] * cos - pvolt[1] * sin)
        stack[pl.ds(0, LINES)] = inward
        stack[pl.ds(LINES, CONV)] = jnp.where(live, axial * cos - normal * sin, 0.0)
        stack[pl.ds(LINES + CONV, PORTS)] = source
        high, low = split(stack[...])
        w[pl.ds(nodes, 128), pl.ds(0, 128)] = high
        w[pl.ds(nodes, 128), pl.ds(128, 128)] = low
        w[pl.ds(nodes + 128, 128), pl.ds(0, 128)] = high
        block = 256
        for i in range(0, nodes, block):
            at = pl.ds(i, block)
            y = dot(g_high[at, :], w[...])
            z = dot(g_low[at, :], w[pl.ds(0, nodes), pl.ds(0, 128)])
            v = y[:, :128] + y[:, 128:] + z
            volt[at, :] = v
            h = cap2[at, :] * v - hist_out[at, :]
            hist_out[at, :] = h
            high, low = split(h)
            w_next[at, pl.ds(0, 128)] = high
            w_next[at, pl.ds(128, 128)] = low
        for base, where in ((0, line_node), (LINES, conv_node), (LINES + CONV, port_node)):
            for k in range(where.shape[1]):
                probe[pl.ds(base + k, 1), :] = volt[pl.ds(where[0, k], 1), :]
        emf = probe[pl.ds(LINES, CONV), :]
        new_axial = axial + rate * (setpoint[0] - axial) - (SAG_FACTOR * cos) * emf
        new_normal = normal + rate * (setpoint[1] - normal) + (SAG_FACTOR * sin) * emf
        state_out[0] = jnp.where(live, limit * jnp.tanh(new_axial * inverse), axial)
        state_out[1] = jnp.where(live, limit * jnp.tanh(new_normal * inverse), normal)
        waves[t] = line_adm * probe[pl.ds(0, LINES), :] - inward
        flow = source - padm * probe[pl.ds(LINES + CONV, PORTS), :]
        current[0] = current[0] + flow * cos
        current[1] = current[1] - flow * sin

    def several(i, _):
        for j in range(0, UNROLL, 2):
            step(UNROLL * i + j, w_even, w_odd)
            step(UNROLL * i + j + 1, w_odd, w_even)
        return 0

    lax.fori_loop(0, STEPS // UNROLL, several, 0)
    current[...] = current[...] * (2.0 / STEPS)


def window(angle, whole_numbers, ginv, hist0, arrivals, gcap, state, setpoint, pvolt, nodes_of, coefficients):
    nodes, cases = hist0.shape
    smem = pl.BlockSpec(memory_space=pltpu.SMEM)
    vmem = pl.BlockSpec(memory_space=pltpu.VMEM)
    chunks = 8
    scalars = (angle, *whole_numbers, *nodes_of)
    far = (ginv, hist0, gcap, state, setpoint, pvolt)
    rows = (*arrivals, *nodes_of, *coefficients)
    return pl.pallas_call(
        window_kernel,
        out_shape=(
            jax.ShapeDtypeStruct((STEPS, LINES, cases), F32),
            jax.ShapeDtypeStruct((nodes, cases), F32),
            jax.ShapeDtypeStruct(state.shape, F32),
            jax.ShapeDtypeStruct((2, PORTS, cases), F32),
        ),
        in_specs=[smem] * len(scalars)
        + [pl.BlockSpec(memory_space=pltpu.HBM)] * len(far)
        + [vmem] * len(rows),
        out_specs=(vmem,) * 4,
        scratch_shapes=[
            pltpu.VMEM((chunks, nodes // chunks, nodes), F32),
            pltpu.VMEM((nodes, nodes + 256), BF16),
            pltpu.VMEM((nodes, nodes), BF16),
            pltpu.VMEM((LINES, HIST, cases), F32),
            pltpu.VMEM((STEPS, LINES, cases), F32),
            pltpu.VMEM((nodes + 256, 256), BF16),
            pltpu.VMEM((nodes + 256, 256), BF16),
            pltpu.VMEM((nodes, cases), F32),
            pltpu.VMEM((PROBES, cases), F32),
            pltpu.VMEM((128, cases), F32),
            pltpu.VMEM((nodes, cases), F32),
            pltpu.VMEM((2, 128, cases), F32),
            pltpu.VMEM(setpoint.shape, F32),
            pltpu.VMEM(pvolt.shape, F32),
            pltpu.VMEM(gcap.shape, F32),
            pltpu.VMEM((8, 128), jnp.int32),
            pltpu.VMEM((8, 128), F32),
            pltpu.SemaphoreType.DMA((chunks,)),
            pltpu.SemaphoreType.DMA((4,)),
            pltpu.SemaphoreType.DMA((5,)),
        ],
        compiler_params=pltpu.CompilerParams(vmem_limit_bytes=59 << 20),
        cost_estimate=pl.CostEstimate(
            flops=6 * STEPS * nodes * nodes * cases,
            bytes_accessed=64 << 20,
            transcendentals=0,
        ),
        name="window",
    )(*scalars, *far, *rows)


def spread_kernel(current, impedance, out):
    for i in range(out.shape[0]):
        out[i] = current[...]


def spread(current, impedance, size):
    vmem = pl.BlockSpec(memory_space=pltpu.VMEM)
    return pl.pallas_call(
        spread_kernel,
        out_shape=jax.ShapeDtypeStruct((size, *current.shape), F32),
        in_specs=[vmem, pl.BlockSpec(memory_space=pl.ANY)],
        out_specs=vmem,
        compiler_params=pltpu.CompilerParams(vmem_limit_bytes=16 << 20),
        name="spread_currents",
    )(current, impedance)


def bus_kernel(place, impedance, own, other, out, gathered):
    chips, areas = own.shape[:2]
    y, core = place[0], place[1]
    for k in range(chips):
        row = lax.rem(y - k + chips, chips) * 2
        for i in range(areas):
            for part in range(2):
                gathered[i, part, row + core] = own[k, i, part]
                gathered[i, part, row + 1 - core] = other[k, i, part]
    rows = pl.ds(0, out.shape[1])
    z = jnp.concatenate([impedance[i, rows, :] for i in range(areas)], axis=1)
    parts = []
    for i in range(areas):
        real = gathered[i, 0].reshape(-1, 128)
        imag = gathered[i, 1].reshape(-1, 128)
        parts.append(jnp.concatenate([real, imag], axis=1))
        parts.append(jnp.concatenate([-imag, real], axis=1))
    w = jnp.concatenate(parts, axis=0)
    z_high, z_low = split(z)
    w_high, w_low = split(w)
    volts = dot(z_high, w_high) + dot(z_low, w_high) + dot(z_high, w_low)
    out[0] = volts[:, :128]
    out[1] = volts[:, 128:]


def bus_product(place, impedance, own, other):
    chips, areas, _, ports, cases = own.shape
    vmem = pl.BlockSpec(memory_space=pltpu.VMEM)
    return pl.pallas_call(
        bus_kernel,
        out_shape=jax.ShapeDtypeStruct((2, impedance.shape[1] - 8, cases), F32),
        in_specs=[pl.BlockSpec(memory_space=pltpu.SMEM)] + [vmem] * 3,
        out_specs=vmem,
        scratch_shapes=[pltpu.VMEM((areas, 2, 2 * chips, ports, cases), F32)],
        compiler_params=pltpu.CompilerParams(vmem_limit_bytes=32 << 20),
        name="bus_product",
    )(place, impedance, own, other)


def sum_kernel(*refs):
    total = refs[0][...]
    for ref in refs[1:-1]:
        total = total + ref[...]
    refs[-1][...] = total


def sum_of(parts):
    vmem = pl.BlockSpec(memory_space=pltpu.VMEM)
    return pl.pallas_call(
        sum_kernel,
        out_shape=jax.ShapeDtypeStruct(parts[0].shape, F32),
        in_specs=[vmem] * len(parts),
        out_specs=vmem,
        compiler_params=pltpu.CompilerParams(vmem_limit_bytes=16 << 20),
        name="sum_of_parts",
    )(*parts)


def port_kernel(first, ports, volts, out):
    rows = volts.shape[1]
    both = jnp.concatenate([volts[0], volts[1]], axis=1)
    high, rest = split(both)
    middle = both - high.astype(F32)
    low = (middle - rest.astype(F32)).astype(BF16)
    row = lax.broadcasted_iota(jnp.int32, (rows, 128), 0) + first[0]
    for area in range(ports.shape[0]):
        wanted = ports[area, pl.ds(rows, 1), :].astype(jnp.int32)
        picks = jnp.where(row == wanted, 1.0, 0.0).T.astype(BF16)
        found = dot(picks, high) + dot(picks, rest) + dot(picks, low)
        for member in range(out.shape[0]):
            out[member, area] = found[member * PORTS : (member + 1) * PORTS]


def port_rows(first, ports, volts, members):
    vmem = pl.BlockSpec(memory_space=pltpu.VMEM)
    return pl.pallas_call(
        port_kernel,
        out_shape=jax.ShapeDtypeStruct((members, ports.shape[0], PORTS, 2 * volts.shape[2]), F32),
        in_specs=[pl.BlockSpec(memory_space=pltpu.SMEM), vmem, vmem],
        out_specs=vmem,
        compiler_params=pltpu.CompilerParams(vmem_limit_bytes=32 << 20),
        name="port_rows",
    )(first, ports, volts)


def shifted(x, by):
    size = lax.axis_size(ALL)
    return lax.ppermute(x, ALL, [(i, (i + by) % size) for i in range(size)])


def copy_kernel(source, target, parts, in_sem, out_sem):
    count, rows, _ = parts.shape
    each = source.shape[1] // rows
    fetches, stores = [], []
    for i in range(count):
        at = pl.ds((i % each) * rows, rows)
        fetches.append(pltpu.make_async_copy(source.at[i // each, at], parts.at[i], in_sem.at[i]))
        stores.append(pltpu.make_async_copy(parts.at[i], target.at[i // each, at], out_sem.at[i]))
    for fetch in fetches:
        fetch.start()
    for fetch, store in zip(fetches, stores):
        fetch.wait()
        store.start()
    for store in stores:
        store.wait()


def copied(x):
    each = 4
    count = x.shape[0] * each
    anywhere = pl.BlockSpec(memory_space=pl.ANY)
    return pl.pallas_call(
        copy_kernel,
        out_shape=jax.ShapeDtypeStruct(x.shape, x.dtype),
        in_specs=[anywhere],
        out_specs=anywhere,
        scratch_shapes=[
            pltpu.VMEM((count, x.shape[1] // each, x.shape[2]), x.dtype),
            pltpu.SemaphoreType.DMA((count,)),
            pltpu.SemaphoreType.DMA((count,)),
        ],
        compiler_params=pltpu.CompilerParams(vmem_limit_bytes=60 << 20),
        name="copy_voltages",
    )(x)


def along(x, axis, by):
    size = lax.axis_size(axis)
    return lax.ppermute(x, axis, [(i, (i + by) % size) for i in range(size)])


def from_all(x, axis):
    near, far, back = (along(x, axis, by) for by in (1, 3, 2))
    return x, near, back, far


def per_device(
    conductance_inverse,
    cap_history,
    cap_conductance,
    wave_history,
    line_partner,
    line_node,
    line_delay,
    line_admittance,
    conv_node,
    conv_count,
    conv_state,
    conv_reference,
    conv_rate,
    conv_limit,
    port_node,
    port_admittance,
    port_voltage_prev,
    port_bus,
    transfer_impedance,
):
    areas = lax.axis_size("z")
    members = lax.axis_size(ROW)
    bus_rows = transfer_impedance.shape[1]
    with jax.named_scope("wave_exchange"):
        near_up, far_down, near_down, far_up = pack(line_partner, wave_history[0])
        from_below = shifted(near_up, 1)
        from_above = shifted(near_down, -1)
        from_far_above = shifted(far_down, -2)
        from_far_below = shifted(far_up, 2)
        arrivals = (from_below, from_far_above, from_above, from_far_below)
    with jax.named_scope("impedance_exchange"):
        blocks = turn(jnp.swapaxes(transfer_impedance, 1, 2), areas)
        ports = port_bus.reshape(1, 1, -1).astype(F32)
        ports = jnp.pad(ports, ((0, 0), (0, 0), (0, 128 - ports.shape[2])), constant_values=-1.0)
        ports = port_block(ports[0], arrivals, areas)
        blocks = lax.dynamic_update_slice(blocks, ports, (0, blocks.shape[1] - 8, 0))
        impedance = lax.all_to_all(blocks, "z", 0, 0, tiled=True)
    with jax.named_scope("window"):
        theta = np.arange(1, STEPS + 1, dtype=np.float32) * np.float32(2.0 * math.pi / STEPS)
        angle = jnp.asarray(np.stack([np.cos(theta), np.sin(theta)]).astype(np.float32))
        outward, hist_end, conv_out, current = window(
            angle,
            (line_partner, line_delay, conv_count),
            conductance_inverse[0],
            cap_history[0],
            arrivals,
            cap_conductance,
            conv_state[0],
            conv_reference[0],
            port_voltage_prev[:, 0],
            (line_node, conv_node, port_node),
            (line_admittance, conv_limit, conv_rate, port_admittance),
        )
    with jax.named_scope("currents"):
        flat = spread(current, impedance, areas)
        flat = lax.all_to_all(flat, "z", 0, 0, tiled=True)
        own = jnp.stack(from_all(flat, "y"))
        other = along(own, "core", 1)
        place = jnp.stack([lax.axis_index("y"), lax.axis_index("core")]).astype(jnp.int32)
    with jax.named_scope("bus_voltage"):
        partial = bus_product(place, impedance, own, other)
        block = sum_of(from_all(partial, "x"))
        bus_voltage = copied(lax.all_gather(block, "z", axis=1, tiled=True))
    with jax.named_scope("port_voltage"):
        first = lax.axis_index(ROW) * bus_rows + lax.axis_index("z") * block.shape[1]
        picked = port_rows(first[None].astype(jnp.int32), impedance, block, members)
        mine = jnp.sum(lax.all_to_all(picked, ROW, 0, 0, tiled=True), axis=0)
        mine = jnp.sum(lax.all_to_all(mine, "z", 0, 0, tiled=True), axis=0)
        cases = mine.shape[1] // 2
        port_voltage = jnp.stack([mine[:, :cases], mine[:, cases:]])[:, None]
    return (outward[None], hist_end[None], conv_out[None], bus_voltage, port_voltage)


def solution(mesh):
    devices = mesh.devices.reshape(8, 4, 4, 2)
    torus = Mesh(devices, ALL)
    return jax.shard_map(
        per_device,
        mesh=torus,
        in_specs=(
            P(ALL, None, None),
            P(ALL, None, None),
            P(ALL, None),
            P(ALL, None, None, None),
            P(ALL, None),
            P(ALL, None),
            P(ALL, None),
            P(ALL, None),
            P(ALL, None),
            P(ALL),
            P(ALL, None, None, None),
            P(ALL, None, None, None),
            P(ALL, None),
            P(ALL, None),
            P(ALL, None),
            P(ALL, None),
            P(None, ALL, None, None),
            P(AREA, None),
            P(None, ROW, AREA),
        ),
        out_specs=(
            P(ALL, None, None, None),
            P(ALL, None, None),
            P(ALL, None, None, None),
            P(None, ROW, None),
            P(None, ALL, None, None),
        ),
        check_vma=False,
    )
```

```python
import math

import jax
import jax.numpy as jnp
import numpy as np
from jax import lax
from jax.experimental import pallas as pl
from jax.experimental.pallas import tpu as pltpu
from jax.sharding import Mesh
from jax.sharding import PartitionSpec as P

STEPS = 20
HIST = 40
NEAR = 12
LINES = 32
CONV = 64
PORTS = 8
HALF = LINES // 2
PROBES = LINES + CONV + PORTS
SAG_FACTOR = 0.3
UNROLL = 4
ALL = ("z", "x", "y", "core")
AREA = ("z", "x")
ROW = ("y", "core")
F32 = jnp.float32
BF16 = jnp.bfloat16


def dot(a, b):
    return jnp.dot(a, b, preferred_element_type=F32)


def split(x):
    high = x.astype(BF16)
    return high, (x - high.astype(F32)).astype(BF16)


def reach_of(partner, line):
    return jnp.bitwise_and(partner[0, line] - partner[0, HALF + line], 255) // 2


def pack_kernel(partner, waves, near_up, far_down, near_down, far_up):
    near = jnp.int32(0)
    for line in range(HALF):
        is_near = reach_of(partner, line) == 1
        up = waves[:, line, :]
        down = waves[:, line + HALF, :]

        @pl.when(is_near)
        def _(near=near, up=up, down=down):
            near_up[near] = up
            near_down[near] = down

        @pl.when(jnp.logical_not(is_near))
        def _(far=line - near, up=up, down=down):
            far_up[far] = up
            far_down[far] = down

        near = near + is_near.astype(jnp.int32)


def pack(partner, waves):
    hist, _, cases = waves.shape
    near = jax.ShapeDtypeStruct((NEAR, hist, cases), F32)
    far = jax.ShapeDtypeStruct((HALF - NEAR, hist, cases), F32)
    vmem = pl.BlockSpec(memory_space=pltpu.VMEM)
    return pl.pallas_call(
        pack_kernel,
        out_shape=(near, far, near, far),
        in_specs=[pl.BlockSpec(memory_space=pltpu.SMEM), vmem],
        out_specs=(vmem,) * 4,
        compiler_params=pltpu.CompilerParams(vmem_limit_bytes=32 << 20),
        name="pack_waves",
    )(partner, waves)


def turn_kernel(impedance, blocks):
    areas, rows, _ = blocks.shape
    rows = rows - 8
    for first in range(0, areas * rows, 128):
        part = impedance[:, :, pl.ds(first, 128)]
        turned = jnp.concatenate([part[0], part[1]], axis=0).T
        done = 0
        while done < 128:
            area, at = divmod(first + done, rows)
            size = min(128 - done, rows - at)
            blocks[area, pl.ds(at, size), :] = turned[done : done + size]
            done += size
    blocks[:, pl.ds(rows, 8), :] = jnp.zeros((areas, 8, 128), F32)


def turn(impedance, areas):
    vmem = pl.BlockSpec(memory_space=pltpu.VMEM)
    return pl.pallas_call(
        turn_kernel,
        out_shape=jax.ShapeDtypeStruct((areas, impedance.shape[2] // areas + 8, 128), F32),
        in_specs=[vmem],
        out_specs=vmem,
        compiler_params=pltpu.CompilerParams(vmem_limit_bytes=32 << 20),
        name="turn_impedance",
    )(impedance)


def port_block_kernel(ports, *rest):
    rest[-1][...] = jnp.broadcast_to(ports[...], rest[-1].shape)


def port_block(ports, before, areas):
    vmem = pl.BlockSpec(memory_space=pltpu.VMEM)
    return pl.pallas_call(
        port_block_kernel,
        out_shape=jax.ShapeDtypeStruct((areas, 8, 128), F32),
        in_specs=[vmem] * (1 + len(before)),
        out_specs=vmem,
        compiler_params=pltpu.CompilerParams(vmem_limit_bytes=16 << 20),
        name="port_block",
    )(ports, *before)


def column(row):
    return jnp.broadcast_to(row, (128, 128)).T


def window_kernel(
    angle,
    partner,
    delay,
    count,
    line_node,
    conv_node,
    port_node,
    g_hbm,
    hist0_hbm,
    gcap_hbm,
    state0_hbm,
    setpoint_hbm,
    pvolt_hbm,
    near_up,
    far_down,
    near_down,
    far_up,
    line_nodes,
    conv_nodes,
    port_nodes,
    line_adms,
    limits,
    rates,
    port_adms,
    waves,
    hist_out,
    state_out,
    current,
    g_in,
    g_high,
    g_low,
    arrived,
    incoming,
    w_even,
    w_odd,
    volt,
    probe,
    stack,
    cap2,
    coef,
    setpoint,
    pvolt,
    gcap,
    nodes_row,
    coef_row,
    g_sem,
    a_sem,
    s_sem,
):
    nodes = g_high.shape[0]
    chunks = g_in.shape[0]
    rows = nodes // chunks
    small = []

    def bring(source, target):
        small.append(pltpu.make_async_copy(source, target, s_sem.at[len(small)]))
        small[-1].start()

    bring(gcap_hbm, gcap)
    bring(hist0_hbm, hist_out)
    bring(state0_hbm, state_out)
    bring(setpoint_hbm, setpoint)
    bring(pvolt_hbm, pvolt)
    copies = [
        pltpu.make_async_copy(g_hbm.at[pl.ds(i * rows, rows)], g_in.at[i], g_sem.at[i])
        for i in range(chunks)
    ]
    for copy in copies:
        copy.start()
    first = 0
    moves = []
    for i, part in enumerate((near_up, far_up, near_down, far_down)):
        size = part.shape[0]
        moves.append(
            pltpu.make_async_copy(part, arrived.at[pl.ds(first, size)], a_sem.at[i])
        )
        first += size
    for move in moves:
        move.start()

    zeros = jnp.zeros((256, 128), BF16)
    for w in (w_even, w_odd):
        w[pl.ds(nodes, 256), pl.ds(0, 128)] = zeros
        w[pl.ds(nodes, 256), pl.ds(128, 128)] = zeros
    current[...] = jnp.zeros_like(current)
    stack[...] = jnp.zeros_like(stack)
    nodes_row[...] = jnp.full(nodes_row.shape, -1, jnp.int32)
    coef_row[...] = jnp.ones(coef_row.shape, F32)
    for copy in small:
        copy.wait()

    at_conv, at_port = pl.ds(LINES, CONV), pl.ds(LINES + CONV, PORTS)
    first_row = pl.ds(0, 1)
    nodes_row[first_row, pl.ds(0, LINES)] = line_nodes[...]
    nodes_row[first_row, at_conv] = conv_nodes[...]
    nodes_row[first_row, at_port] = port_nodes[...]
    coef_row[first_row, pl.ds(0, LINES)] = line_adms[...]
    coef_row[first_row, at_conv] = limits[...]
    coef_row[first_row, at_port] = port_adms[...]
    coef_row[pl.ds(1, 1), at_conv] = rates[...]
    coef[0] = column(coef_row[pl.ds(0, 1), :])
    coef[1] = column(coef_row[pl.ds(1, 1), :])
    for i in range(nodes // 128):
        cap2[pl.ds(i * 128, 128)] = 2.0 * column(gcap[:, pl.ds(i * 128, 128)])
    high, low = split(hist_out[...])
    w_even[pl.ds(0, nodes), pl.ds(0, 128)] = high
    w_even[pl.ds(0, nodes), pl.ds(128, 128)] = low

    picks = (
        lax.broadcasted_iota(jnp.int32, (nodes, 128), 0) == nodes_row[pl.ds(0, 1), :]
    ).astype(BF16)
    for i, copy in enumerate(copies):
        copy.wait()
        high, low = split(g_in[i])
        at = pl.ds(i * rows, rows)
        g_high[at, pl.ds(0, nodes)] = high
        g_low[at, :] = low

    half = nodes // 2
    for i in range(0, nodes, half):
        at = pl.ds(i, half)
        g_high[at, pl.ds(nodes, 128)] = dot(g_high[at, pl.ds(0, nodes)], picks).astype(BF16)
        g_high[at, pl.ds(nodes + 128, 128)] = dot(g_low[at, :], picks).astype(BF16)

    for move in moves:
        move.wait()
    near = jnp.int32(0)
    for line in range(HALF):
        is_near = reach_of(partner, line) == 1
        place = jnp.where(is_near, near, NEAR + line - near)
        near = near + is_near.astype(jnp.int32)
        for slot, at in ((line + HALF, place), (line, place + HALF)):
            start = HIST - delay[0, slot]
            incoming[:, slot, :] = arrived[at, pl.ds(start, STEPS), :]

    line_adm = 2.0 * coef[0, :LINES]
    limit = coef[0, LINES : LINES + CONV]
    padm = coef[0, LINES + CONV : PROBES]
    rate = coef[1, LINES : LINES + CONV]
    inverse = 1.0 / limit
    live = lax.broadcasted_iota(jnp.int32, (CONV, 128), 0) < count[0]

    def step(t, w, w_next):
        cos, sin = angle[0, t], angle[1, t]
        axial, normal = state_out[0], state_out[1]
        inward = incoming[t]
        source = padm * (pvolt[0] * cos - pvolt[1] * sin)
        stack[pl.ds(0, LINES)] = inward
        stack[pl.ds(LINES, CONV)] = jnp.where(live, axial * cos - normal * sin, 0.0)
        stack[pl.ds(LINES + CONV, PORTS)] = source
        high, low = split(stack[...])
        w[pl.ds(nodes, 128), pl.ds(0, 128)] = high
        w[pl.ds(nodes, 128), pl.ds(128, 128)] = low
        w[pl.ds(nodes + 128, 128), pl.ds(0, 128)] = high
        block = 256
        for i in range(0, nodes, block):
            at = pl.ds(i, block)
            y = dot(g_high[at, :], w[...])
            z = dot(g_low[at, :], w[pl.ds(0, nodes), pl.ds(0, 128)])
            v = y[:, :128] + y[:, 128:] + z
            volt[at, :] = v
            h = cap2[at, :] * v - hist_out[at, :]
            hist_out[at, :] = h
            high, low = split(h)
            w_next[at, pl.ds(0, 128)] = high
            w_next[at, pl.ds(128, 128)] = low
        for base, where in ((0, line_node), (LINES, conv_node), (LINES + CONV, port_node)):
            for k in range(where.shape[1]):
                probe[pl.ds(base + k, 1), :] = volt[pl.ds(where[0, k], 1), :]
        emf = probe[pl.ds(LINES, CONV), :]
        new_axial = axial + rate * (setpoint[0] - axial) - (SAG_FACTOR * cos) * emf
        new_normal = normal + rate * (setpoint[1] - normal) + (SAG_FACTOR * sin) * emf
        state_out[0] = jnp.where(live, limit * jnp.tanh(new_axial * inverse), axial)
        state_out[1] = jnp.where(live, limit * jnp.tanh(new_normal * inverse), normal)
        waves[t] = line_adm * probe[pl.ds(0, LINES), :] - inward
        flow = source - padm * probe[pl.ds(LINES + CONV, PORTS), :]
        current[0] = current[0] + flow * cos
        current[1] = current[1] - flow * sin

    def several(i, _):
        for j in range(0, UNROLL, 2):
            step(UNROLL * i + j, w_even, w_odd)
            step(UNROLL * i + j + 1, w_odd, w_even)
        return 0

    lax.fori_loop(0, STEPS // UNROLL, several, 0)
    current[...] = current[...] * (2.0 / STEPS)


def window(angle, whole_numbers, ginv, hist0, arrivals, gcap, state, setpoint, pvolt, nodes_of, coefficients):
    nodes, cases = hist0.shape
    smem = pl.BlockSpec(memory_space=pltpu.SMEM)
    vmem = pl.BlockSpec(memory_space=pltpu.VMEM)
    chunks = 8
    scalars = (angle, *whole_numbers, *nodes_of)
    far = (ginv, hist0, gcap, state, setpoint, pvolt)
    rows = (*arrivals, *nodes_of, *coefficients)
    return pl.pallas_call(
        window_kernel,
        out_shape=(
            jax.ShapeDtypeStruct((STEPS, LINES, cases), F32),
            jax.ShapeDtypeStruct((nodes, cases), F32),
            jax.ShapeDtypeStruct(state.shape, F32),
            jax.ShapeDtypeStruct((2, PORTS, cases), F32),
        ),
        in_specs=[smem] * len(scalars)
        + [pl.BlockSpec(memory_space=pltpu.HBM)] * len(far)
        + [vmem] * len(rows),
        out_specs=(vmem,) * 4,
        scratch_shapes=[
            pltpu.VMEM((chunks, nodes // chunks, nodes), F32),
            pltpu.VMEM((nodes, nodes + 256), BF16),
            pltpu.VMEM((nodes, nodes), BF16),
            pltpu.VMEM((LINES, HIST, cases), F32),
            pltpu.VMEM((STEPS, LINES, cases), F32),
            pltpu.VMEM((nodes + 256, 256), BF16),
            pltpu.VMEM((nodes + 256, 256), BF16),
            pltpu.VMEM((nodes, cases), F32),
            pltpu.VMEM((PROBES, cases), F32),
            pltpu.VMEM((128, cases), F32),
            pltpu.VMEM((nodes, cases), F32),
            pltpu.VMEM((2, 128, cases), F32),
            pltpu.VMEM(setpoint.shape, F32),
            pltpu.VMEM(pvolt.shape, F32),
            pltpu.VMEM(gcap.shape, F32),
            pltpu.VMEM((8, 128), jnp.int32),
            pltpu.VMEM((8, 128), F32),
            pltpu.SemaphoreType.DMA((chunks,)),
            pltpu.SemaphoreType.DMA((4,)),
            pltpu.SemaphoreType.DMA((5,)),
        ],
        compiler_params=pltpu.CompilerParams(vmem_limit_bytes=59 << 20),
        cost_estimate=pl.CostEstimate(
            flops=6 * STEPS * nodes * nodes * cases,
            bytes_accessed=64 << 20,
            transcendentals=0,
        ),
        name="window",
    )(*scalars, *far, *rows)


def spread_kernel(current, impedance, out):
    for i in range(out.shape[0]):
        out[i] = current[...]


def spread(current, impedance, size):
    vmem = pl.BlockSpec(memory_space=pltpu.VMEM)
    return pl.pallas_call(
        spread_kernel,
        out_shape=jax.ShapeDtypeStruct((size, *current.shape), F32),
        in_specs=[vmem, pl.BlockSpec(memory_space=pl.ANY)],
        out_specs=vmem,
        compiler_params=pltpu.CompilerParams(vmem_limit_bytes=16 << 20),
        name="spread_currents",
    )(current, impedance)


def bus_kernel(place, impedance, own, other, out, gathered):
    chips, areas = own.shape[:2]
    y, core = place[0], place[1]
    for k in range(chips):
        row = lax.rem(y - k + chips, chips) * 2
        for i in range(areas):
            for part in range(2):
                gathered[i, part, row + core] = own[k, i, part]
                gathered[i, part, row + 1 - core] = other[k, i, part]
    rows = pl.ds(0, out.shape[1])
    z = jnp.concatenate([impedance[i, rows, :] for i in range(areas)], axis=1)
    parts = []
    for i in range(areas):
        real = gathered[i, 0].reshape(-1, 128)
        imag = gathered[i, 1].reshape(-1, 128)
        parts.append(jnp.concatenate([real, imag], axis=1))
        parts.append(jnp.concatenate([-imag, real], axis=1))
    w = jnp.concatenate(parts, axis=0)
    z_high, z_low = split(z)
    w_high, w_low = split(w)
    volts = dot(z_high, w_high) + dot(z_low, w_high) + dot(z_high, w_low)
    out[0] = volts[:, :128]
    out[1] = volts[:, 128:]


def bus_product(place, impedance, own, other):
    chips, areas, _, ports, cases = own.shape
    vmem = pl.BlockSpec(memory_space=pltpu.VMEM)
    return pl.pallas_call(
        bus_kernel,
        out_shape=jax.ShapeDtypeStruct((2, impedance.shape[1] - 8, cases), F32),
        in_specs=[pl.BlockSpec(memory_space=pltpu.SMEM)] + [vmem] * 3,
        out_specs=vmem,
        scratch_shapes=[pltpu.VMEM((areas, 2, 2 * chips, ports, cases), F32)],
        compiler_params=pltpu.CompilerParams(vmem_limit_bytes=32 << 20),
        name="bus_product",
    )(place, impedance, own, other)


def sum_kernel(*refs):
    total = refs[0][...]
    for ref in refs[1:-1]:
        total = total + ref[...]
    refs[-1][...] = total


def sum_of(parts):
    vmem = pl.BlockSpec(memory_space=pltpu.VMEM)
    return pl.pallas_call(
        sum_kernel,
        out_shape=jax.ShapeDtypeStruct(parts[0].shape, F32),
        in_specs=[vmem] * len(parts),
        out_specs=vmem,
        compiler_params=pltpu.CompilerParams(vmem_limit_bytes=16 << 20),
        name="sum_of_parts",
    )(*parts)


def port_kernel(first, ports, volts, out):
    rows = volts.shape[1]
    both = jnp.concatenate([volts[0], volts[1]], axis=1)
    high, rest = split(both)
    middle = both - high.astype(F32)
    low = (middle - rest.astype(F32)).astype(BF16)
    row = lax.broadcasted_iota(jnp.int32, (rows, 128), 0) + first[0]
    for area in range(ports.shape[0]):
        wanted = ports[area, pl.ds(rows, 1), :].astype(jnp.int32)
        picks = jnp.where(row == wanted, 1.0, 0.0).T.astype(BF16)
        found = dot(picks, high) + dot(picks, rest) + dot(picks, low)
        for member in range(out.shape[0]):
            out[member, area] = found[member * PORTS : (member + 1) * PORTS]


def port_rows(first, ports, volts, members):
    vmem = pl.BlockSpec(memory_space=pltpu.VMEM)
    return pl.pallas_call(
        port_kernel,
        out_shape=jax.ShapeDtypeStruct((members, ports.shape[0], PORTS, 2 * volts.shape[2]), F32),
        in_specs=[pl.BlockSpec(memory_space=pltpu.SMEM), vmem, vmem],
        out_specs=vmem,
        compiler_params=pltpu.CompilerParams(vmem_limit_bytes=32 << 20),
        name="port_rows",
    )(first, ports, volts)


def shifted(x, by):
    size = lax.axis_size(ALL)
    return lax.ppermute(x, ALL, [(i, (i + by) % size) for i in range(size)])


def place_kernel(source, target, parts, in_sem, out_sem):
    areas, halves, rows, _ = source.shape
    fetches, stores = [], []
    for i in range(areas * halves):
        area, half = divmod(i, halves)
        at = target.at[half, pl.ds(area * rows, rows)]
        fetches.append(pltpu.make_async_copy(source.at[area, half], parts.at[i], in_sem.at[i]))
        stores.append(pltpu.make_async_copy(parts.at[i], at, out_sem.at[i]))
    for fetch in fetches:
        fetch.start()
    for fetch, store in zip(fetches, stores):
        fetch.wait()
        store.start()
    for store in stores:
        store.wait()


def placed(x):
    areas, halves, rows, cases = x.shape
    count = areas * halves
    anywhere = pl.BlockSpec(memory_space=pl.ANY)
    return pl.pallas_call(
        place_kernel,
        out_shape=jax.ShapeDtypeStruct((halves, areas * rows, cases), x.dtype),
        in_specs=[anywhere],
        out_specs=anywhere,
        scratch_shapes=[
            pltpu.VMEM((count, rows, cases), x.dtype),
            pltpu.SemaphoreType.DMA((count,)),
            pltpu.SemaphoreType.DMA((count,)),
        ],
        compiler_params=pltpu.CompilerParams(vmem_limit_bytes=60 << 20),
        name="place_voltages",
    )(x)


def along(x, axis, by):
    size = lax.axis_size(axis)
    return lax.ppermute(x, axis, [(i, (i + by) % size) for i in range(size)])


def from_all(x, axis):
    near, far, back = (along(x, axis, by) for by in (1, 3, 2))
    return x, near, back, far


def per_device(
    conductance_inverse,
    cap_history,
    cap_conductance,
    wave_history,
    line_partner,
    line_node,
    line_delay,
    line_admittance,
    conv_node,
    conv_count,
    conv_state,
    conv_reference,
    conv_rate,
    conv_limit,
    port_node,
    port_admittance,
    port_voltage_prev,
    port_bus,
    transfer_impedance,
):
    areas = lax.axis_size("z")
    members = lax.axis_size(ROW)
    bus_rows = transfer_impedance.shape[1]
    with jax.named_scope("wave_exchange"):
        near_up, far_down, near_down, far_up = pack(line_partner, wave_history[0])
        from_below = shifted(near_up, 1)
        from_above = shifted(near_down, -1)
        from_far_above = shifted(far_down, -2)
        from_far_below = shifted(far_up, 2)
        arrivals = (from_below, from_far_above, from_above, from_far_below)
    with jax.named_scope("impedance_exchange"):
        blocks = turn(jnp.swapaxes(transfer_impedance, 1, 2), areas)
        ports = port_bus.reshape(1, 1, -1).astype(F32)
        ports = jnp.pad(ports, ((0, 0), (0, 0), (0, 128 - ports.shape[2])), constant_values=-1.0)
        ports = port_block(ports[0], arrivals, areas)
        blocks = lax.dynamic_update_slice(blocks, ports, (0, blocks.shape[1] - 8, 0))
        impedance = lax.all_to_all(blocks, "z", 0, 0, tiled=True)
    with jax.named_scope("window"):
        theta = np.arange(1, STEPS + 1, dtype=np.float32) * np.float32(2.0 * math.pi / STEPS)
        angle = jnp.asarray(np.stack([np.cos(theta), np.sin(theta)]).astype(np.float32))
        outward, hist_end, conv_out, current = window(
            angle,
            (line_partner, line_delay, conv_count),
            conductance_inverse[0],
            cap_history[0],
            arrivals,
            cap_conductance,
            conv_state[0],
            conv_reference[0],
            port_voltage_prev[:, 0],
            (line_node, conv_node, port_node),
            (line_admittance, conv_limit, conv_rate, port_admittance),
        )
    with jax.named_scope("currents"):
        flat = spread(current, impedance, areas)
        flat = lax.all_to_all(flat, "z", 0, 0, tiled=True)
        own = jnp.stack(from_all(flat, "y"))
        other = along(own, "core", 1)
        place = jnp.stack([lax.axis_index("y"), lax.axis_index("core")]).astype(jnp.int32)
    with jax.named_scope("bus_voltage"):
        partial = bus_product(place, impedance, own, other)
        block = sum_of(from_all(partial, "x"))
        bus_voltage = placed(lax.all_gather(block, "z"))
    with jax.named_scope("port_voltage"):
        first = lax.axis_index(ROW) * bus_rows + lax.axis_index("z") * block.shape[1]
        picked = port_rows(first[None].astype(jnp.int32), impedance, block, members)
        mine = jnp.sum(lax.all_to_all(picked, ROW, 0, 0, tiled=True), axis=0)
        mine = jnp.sum(lax.all_to_all(mine, "z", 0, 0, tiled=True), axis=0)
        cases = mine.shape[1] // 2
        port_voltage = jnp.stack([mine[:, :cases], mine[:, cases:]])[:, None]
    return (outward[None], hist_end[None], conv_out[None], bus_voltage, port_voltage)


def solution(mesh):
    devices = mesh.devices.reshape(8, 4, 4, 2)
    torus = Mesh(devices, ALL)
    return jax.shard_map(
        per_device,
        mesh=torus,
        in_specs=(
            P(ALL, None, None),
            P(ALL, None, None),
            P(ALL, None),
            P(ALL, None, None, None),
            P(ALL, None),
            P(ALL, None),
            P(ALL, None),
            P(ALL, None),
            P(ALL, None),
            P(ALL),
            P(ALL, None, None, None),
            P(ALL, None, None, None),
            P(ALL, None),
            P(ALL, None),
            P(ALL, None),
            P(ALL, None),
            P(None, ALL, None, None),
            P(AREA, None),
            P(None, ROW, AREA),
        ),
        out_specs=(
            P(ALL, None, None, None),
            P(ALL, None, None),
            P(ALL, None, None, None),
            P(None, ROW, None),
            P(None, ALL, None, None),
        ),
        check_vma=False,
    )
```
